256 devices in a mesh: tensor: 4 (over z_hi, core), section: 64 (over y, x, z_lo).
Axes of the slice: x: 4, y: 4, z: 8 (z_hi: 2, z_lo: 4; z = z_hi * 4 + z_lo), core: 2. Of those that a mesh axis runs over, the one named last changes fastest.
Arguments:
- prompt_lengths: int32 [2], replicated, may hold values from 1024 to 4096, as said below
- owners: int32 [2], replicated, may hold values from 0 to 63, as said below
- span_q: bfloat16 [2, 2048, 64, 128], P(None, ('tensor', 'section')), may hold values from -22 to 22
- span_k: bfloat16 [2, 2048, 8, 128], P(None, ('tensor', 'section')), may hold values from -6 to 6
- span_v: bfloat16 [2, 2048, 8, 128], P(None, ('tensor', 'section')), may hold values from -6 to 6
- prompt_keys: bfloat16 [2, 4096, 8, 128], P(None, 'section', 'tensor'), may hold values from -6 to 6
- prompt_values: bfloat16 [2, 4096, 8, 128], P(None, 'section', 'tensor'), may hold values from -6 to 6
- res_lengths: int32 [256], P('section'), may hold values from 1 to 1024, as said below
- res_keys: bfloat16 [256, 1024, 8, 128], P('section', None, 'tensor'), may hold values from -6 to 6
- res_values: bfloat16 [256, 1024, 8, 128], P('section', None, 'tensor'), may hold values from -6 to 6
- dec_q: bfloat16 [256, 4, 64, 128], P('section', None, 'tensor'), may hold values from -22 to 22
- dec_k: bfloat16 [256, 4, 8, 128], P('section', None, 'tensor'), may hold values from -6 to 6
- dec_v: bfloat16 [256, 4, 8, 128], P('section', None, 'tensor'), may hold values from -6 to 6
- hand_q: bfloat16 [64, 4, 64, 128], P('section', None, 'tensor'), may hold values from -22 to 22
- hand_k: bfloat16 [64, 4, 8, 128], P('section', None, 'tensor'), may hold values from -6 to 6
- hand_v: bfloat16 [64, 4, 8, 128], P('section', None, 'tensor'), may hold values from -6 to 6
Outputs:
- prefill_out: bfloat16 [2, 2048, 64, 128], P(None, ('tensor', 'section'))
- res_out: bfloat16 [256, 4, 64, 128], P('section', None, 'tensor')
- hand_out: bfloat16 [64, 4, 64, 128], P('section', None, 'tensor')
The draws below stay inside these ranges and needn't reach their ends.
Inputs may be any that keep to these rules, and one draw needn't show every extreme that they name: `prompt_lengths`: one prompt has exactly 4096 cached positions. The 2 owners are different slots, and one prompt is handed to slot 63. `res_lengths`: some decode row has exactly 1024 cached positions.
All inputs are finite; a program needn't handle non-finite values.
Results may differ from the reference program's by a relative error of at most 0.013.
Values may be sent and summed in bfloat16 or wider, within the bound.
A program may use at most 128 MiB of HBM per device.

```python
import jax
import jax.numpy as jnp
from jax import lax

HD = 128
QH = 64
KVH = 8
SEQS = 2
RCACHE = 1024
STEPS = 4
SPAN = 2048
PROMPT = 4096
RES_ROWS = 256
SLOTS = 64


def signs_of(base_key):
    return jnp.where(jax.random.bernoulli(base_key, 0.5, (KVH, HD)), 1.0, -1.0).astype(jnp.float32)


def keys_with(key, shape):
    noise = jax.random.truncated_normal(key, -6.0, 6.0, shape, jnp.float32)
    return noise


def queries_with(shared, key, shape, share, low, high):
    noise_key, pick_key, size_key = jax.random.split(key, 3)
    noise = jax.random.truncated_normal(noise_key, -6.0, 6.0, shape, jnp.float32)
    chosen = jax.random.bernoulli(pick_key, share, shape[:-1])
    strength = jax.random.uniform(size_key, shape[:-1], jnp.float32, low, high)
    leaning = jnp.repeat(shared, shape[-2] // shared.shape[0], axis=0)
    aligned = strength[..., None] * leaning + 0.3 * noise
    return jnp.where(chosen[..., None], aligned, noise)


def draw_prompt_lengths(key, part):
    key = jax.random.fold_in(key, 11)
    first_key, pick_key = jax.random.split(key)
    lengths = jax.random.randint(first_key, (SEQS,), PROMPT // 4, PROMPT + 1, dtype=jnp.int32)
    longest = jax.random.randint(pick_key, (), 0, SEQS, dtype=jnp.int32)
    return jnp.where(jnp.arange(SEQS, dtype=jnp.int32) == longest, PROMPT, lengths).astype(jnp.int32)


def draw_owners(key, part):
    key = jax.random.fold_in(key, 12)
    order_key, pick_key = jax.random.split(key)
    others = jax.random.permutation(order_key, max(SLOTS - 1, 1))
    others = jnp.concatenate([others, jnp.zeros((SEQS,), jnp.int32)])[:SEQS].astype(jnp.int32)
    chosen = jax.random.randint(pick_key, (), 0, SEQS, dtype=jnp.int32)
    return jnp.where(jnp.arange(SEQS, dtype=jnp.int32) == chosen, SLOTS - 1, others).astype(jnp.int32)


def draw_res_lengths(key, part):
    key = jax.random.fold_in(key, 13)
    first_key, pick_key = jax.random.split(key)
    lengths = jax.random.randint(first_key, (RES_ROWS,), 1, RCACHE + 1, dtype=jnp.int32)
    longest = jax.random.randint(pick_key, (), 0, RES_ROWS, dtype=jnp.int32)
    return jnp.where(jnp.arange(RES_ROWS, dtype=jnp.int32) == longest, RCACHE, lengths).astype(jnp.int32)


def draw_span_q(key, part):
    shared = signs_of(key)
    key = jax.random.fold_in(key, 21)
    return queries_with(shared, key, (SEQS, SPAN, QH, HD), 0.0, 0.0, 1.0).astype(jnp.bfloat16)


def draw_dec_q(key, part):
    shared = signs_of(key)
    key = jax.random.fold_in(key, 22)
    return queries_with(shared, key, (RES_ROWS, STEPS, QH, HD), 0.0, 0.0, 1.0).astype(jnp.bfloat16)


def draw_hand_q(key, part):
    shared = signs_of(key)
    key = jax.random.fold_in(key, 23)
    return queries_with(shared, key, (SLOTS, STEPS, QH, HD), 0.0, 0.0, 1.0).astype(jnp.bfloat16)


def draw_span_k(key, part):
    key = jax.random.fold_in(key, 31)
    return keys_with(key, (SEQS, SPAN, KVH, HD)).astype(jnp.bfloat16)


def draw_prompt_keys(key, part):
    key = jax.random.fold_in(key, 32)
    return keys_with(key, (SEQS, PROMPT, KVH, HD)).astype(jnp.bfloat16)


def draw_res_keys(key, part):
    key = jax.random.fold_in(key, 33)
    return keys_with(key, (RES_ROWS, RCACHE, KVH, HD)).astype(jnp.bfloat16)


def draw_dec_k(key, part):
    key = jax.random.fold_in(key, 34)
    return keys_with(key, (RES_ROWS, STEPS, KVH, HD)).astype(jnp.bfloat16)


def draw_hand_k(key, part):
    key = jax.random.fold_in(key, 35)
    return keys_with(key, (SLOTS, STEPS, KVH, HD)).astype(jnp.bfloat16)


def shard_levels(own_key, shape, cuts, smallest, top_value):
    def one(position, blocks):
        draws = jax.random.uniform(jax.random.fold_in(jax.random.fold_in(own_key, 6), position), (blocks,), jnp.float32, smallest / len(cuts), top_value / len(cuts))
        return jnp.repeat(jnp.exp(draws), shape[position] // blocks).reshape((-1,) + (1,) * (len(shape) - position - 1))

    gain = one(*cuts[0])
    for cut in cuts[1:]:
        gain = gain * one(*cut)
    return gain


def centred(own_key, shape, deviation, bound, cuts=(), kind=jnp.bfloat16):
    entries = deviation * jax.random.normal(own_key, shape, jnp.float32)
    if cuts:
        entries = entries * shard_levels(own_key, shape, cuts, -0.22, 0.18)
    return jnp.clip(entries, -bound, bound).astype(kind)


def setup_inputs(seed: int = 0) -> dict:
    key_list = jax.random.split(jax.random.key(seed), 17)
    prompt_lengths = draw_prompt_lengths(jax.random.fold_in(key_list[16], 71), 0)
    owners = draw_owners(jax.random.fold_in(key_list[16], 71), 0)
    span_q = draw_span_q(jax.random.fold_in(key_list[16], 71), 0)
    span_k = draw_span_k(jax.random.fold_in(key_list[16], 71), 0)
    span_v = centred(key_list[4], (SEQS, SPAN, KVH, HD), 1.0, 6.0, ((1, 256),))
    prompt_keys = draw_prompt_keys(jax.random.fold_in(key_list[16], 71), 0)
    prompt_values = centred(key_list[6], (SEQS, PROMPT, KVH, HD), 1.0, 6.0, ((1, 64), (2, 4)))
    res_lengths = draw_res_lengths(jax.random.fold_in(key_list[16], 71), 0)
    res_keys = draw_res_keys(jax.random.fold_in(key_list[16], 71), 0)
    res_values = centred(key_list[9], (RES_ROWS, RCACHE, KVH, HD), 1.0, 6.0, ((0, 64), (2, 4)))
    dec_q = draw_dec_q(jax.random.fold_in(key_list[16], 71), 0)
    dec_k = draw_dec_k(jax.random.fold_in(key_list[16], 71), 0)
    dec_v = centred(key_list[12], (RES_ROWS, STEPS, KVH, HD), 1.0, 6.0, ((0, 64), (2, 4)))
    hand_q = draw_hand_q(jax.random.fold_in(key_list[16], 71), 0)
    hand_k = draw_hand_k(jax.random.fold_in(key_list[16], 71), 0)
    hand_v = centred(key_list[15], (SLOTS, STEPS, KVH, HD), 1.0, 6.0, ((0, 64), (2, 4)))
    return {"prompt_lengths": prompt_lengths, "owners": owners, "span_q": span_q, "span_k": span_k, "span_v": span_v, "prompt_keys": prompt_keys, "prompt_values": prompt_values, "res_lengths": res_lengths, "res_keys": res_keys, "res_values": res_values, "dec_q": dec_q, "dec_k": dec_k, "dec_v": dec_v, "hand_q": hand_q, "hand_k": hand_k, "hand_v": hand_v}


def attend(queries, keys_here, values_here, valid_keys):
    score_scale = HD ** -0.5
    scores = jnp.dot(queries, keys_here.T, preferred_element_type=jnp.float32) * score_scale
    scores = jnp.where(valid_keys, scores, -1e30)
    row_top = jnp.max(scores, axis=-1, keepdims=True)
    weights = jnp.where(valid_keys, jnp.exp(scores - row_top), 0.0)
    weight_sum = jnp.sum(weights, axis=-1, keepdims=True)
    mixed_sum = jnp.dot(weights.astype(jnp.bfloat16), values_here, preferred_element_type=jnp.float32)
    return (mixed_sum / weight_sum).astype(jnp.bfloat16)


def prefill(span_q, span_k, span_v, prompt_keys, prompt_values, prompt_lengths):
    group_size = QH // KVH
    span_order = jnp.arange(SPAN, dtype=jnp.int32)
    causal = span_order[None, :] <= span_order[:, None]

    def attend_one(flat_index):
        seq_index = flat_index // QH
        head_index = flat_index % QH
        kv_head = head_index // group_size
        keys_seq = jnp.concatenate([prompt_keys[seq_index, :, kv_head, :], span_k[seq_index, :, kv_head, :]], axis=0)
        values_seq = jnp.concatenate([prompt_values[seq_index, :, kv_head, :], span_v[seq_index, :, kv_head, :]], axis=0)
        prompt_ok = jnp.arange(PROMPT, dtype=jnp.int32) < prompt_lengths[seq_index]
        valid_keys = jnp.concatenate([jnp.broadcast_to(prompt_ok[None, :], (SPAN, PROMPT)), causal], axis=1)
        return attend(span_q[seq_index, :, head_index, :], keys_seq, values_seq, valid_keys)

    results = lax.map(attend_one, jnp.arange(SEQS * QH, dtype=jnp.int32))
    return results.reshape(SEQS, QH, SPAN, HD).transpose(0, 2, 1, 3)


def resident(res_lengths, res_keys, res_values, dec_q, dec_k, dec_v):
    group_size = QH // KVH
    step_order = jnp.arange(STEPS, dtype=jnp.int32)
    step_valid = step_order[None, :] <= step_order[:, None]

    def attend_row(row_index):
        cache_ok = jnp.arange(RCACHE, dtype=jnp.int32) < res_lengths[row_index]
        valid_keys = jnp.concatenate([jnp.broadcast_to(cache_ok[None, :], (STEPS, RCACHE)), step_valid], axis=1)
        keys_row = jnp.concatenate([res_keys[row_index], dec_k[row_index]], axis=0)
        values_row = jnp.concatenate([res_values[row_index], dec_v[row_index]], axis=0)

        def attend_head(head_index):
            kv_head = head_index // group_size
            return attend(dec_q[row_index, :, head_index, :], keys_row[:, kv_head, :], values_row[:, kv_head, :], valid_keys)

        return lax.map(attend_head, jnp.arange(QH, dtype=jnp.int32))

    results = lax.map(attend_row, jnp.arange(RES_ROWS, dtype=jnp.int32))
    return results.transpose(0, 2, 1, 3)


def handed(prompt_lengths, owners, span_k, span_v, prompt_keys, prompt_values, hand_q, hand_k, hand_v):
    group_size = QH // KVH
    step_order = jnp.arange(STEPS, dtype=jnp.int32)
    step_valid = step_order[None, :] <= step_order[:, None]
    result = jnp.zeros((SLOTS, STEPS, QH, HD), jnp.bfloat16)
    for seq_index in range(SEQS):
        owner_slot = owners[seq_index]
        prompt_ok = jnp.arange(PROMPT, dtype=jnp.int32) < prompt_lengths[seq_index]
        valid_keys = jnp.concatenate([jnp.broadcast_to(prompt_ok[None, :], (STEPS, PROMPT)), jnp.ones((STEPS, SPAN), dtype=bool), step_valid], axis=1)
        keys_seq = jnp.concatenate([prompt_keys[seq_index], span_k[seq_index], hand_k[owner_slot]], axis=0)
        values_seq = jnp.concatenate([prompt_values[seq_index], span_v[seq_index], hand_v[owner_slot]], axis=0)
        queries_seq = hand_q[owner_slot]

        def attend_head(head_index):
            kv_head = head_index // group_size
            return attend(queries_seq[:, head_index, :], keys_seq[:, kv_head, :], values_seq[:, kv_head, :], valid_keys)

        results = lax.map(attend_head, jnp.arange(QH, dtype=jnp.int32))
        result = result.at[owner_slot].set(results.transpose(1, 0, 2))
    return result


def reference(prompt_lengths, owners, span_q, span_k, span_v, prompt_keys, prompt_values, res_lengths, res_keys, res_values, dec_q, dec_k, dec_v, hand_q, hand_k, hand_v):
    prefill_out = prefill(span_q, span_k, span_v, prompt_keys, prompt_values, prompt_lengths)
    res_out = resident(res_lengths, res_keys, res_values, dec_q, dec_k, dec_v)
    hand_out = handed(prompt_lengths, owners, span_k, span_v, prompt_keys, prompt_values, hand_q, hand_k, hand_v)
    return (prefill_out, res_out, hand_out)
```

```python
import jax
import jax.numpy as jnp
from jax import lax
from jax.experimental import pallas as pl
from jax.experimental.pallas import tpu as pltpu
from jax.sharding import PartitionSpec as P

MESH = pl.DeviceIdType.MESH
F32 = jnp.float32
BF16 = jnp.bfloat16
SCALE = 128 ** -0.5 * 1.4426950408889634
LOW = -1e30
ROWS = 512


def device_at(x, y, z, c):
    return ((z // 4) * 2 + c, y * 16 + x * 4 + z % 4)


def dot_t(a, b):
    return lax.dot_general(a, b, (((1,), (1,)), ((), ())), preferred_element_type=F32)


def dot(a, b):
    return jnp.dot(a, b, preferred_element_type=F32)


def kernel(
    plen, owners, rlen, span_q, span_k, span_v, prompt_k, prompt_v, res_k, res_v,
    dec_q, dec_k, dec_v, hand_q, hand_k, hand_v,
    out_p, out_r, out_h,
    in_q, in_k, in_v, in_pk, in_pv, in_rk, in_rv,
    wide, stq, rcq, stp, rcp, kv, top, total, mixed, dmat, sto, rco, sth, rch,
    outbuf, resbuf, dkpad, dvpad,
    sem_in, sem_rk, sem_rv, sem_out,
    q_send, q_recv, p_send, p_recv, ring_send, ring_recv, sib_send, sib_recv,
    o_send, o_recv, h_send, h_recv,
):
    t = lax.axis_index("tensor")
    s = lax.axis_index("section")
    zh, c = t // 2, t % 2
    x, y, zl = (s // 4) % 4, s // 16, s % 4
    z = zh * 4 + zl
    j = s // 4
    seq, half = y // 2, y % 2

    def copy_in(a, b, sem):
        cp = pltpu.make_async_copy(a, b, sem)
        cp.start()
        return cp

    cps_p = [copy_in(prompt_k, in_pk, sem_in.at[0]), copy_in(prompt_v, in_pv, sem_in.at[1])]
    cps_s = [
        copy_in(span_k, in_k, sem_in.at[2]),
        copy_in(span_v, in_v, sem_in.at[3]),
        copy_in(span_q, in_q, sem_in.at[4]),
    ]
    cps_k = [copy_in(res_k.at[r], in_rk.at[r], sem_rk.at[r]) for r in range(4)]
    cps_v = [copy_in(res_v.at[r], in_rv.at[r], sem_rv.at[r]) for r in range(4)]

    def column(jj):
        return device_at(jj % 4, jj // 4, z, c)

    up = device_at(x, y, (z + 1) % 8, c)
    down = device_at(x, y, (z + 7) % 8, c)
    sib = device_at(x, y, z, 1 - c)

    p_dest = []
    for sq in range(2):
        for hl in range(2):
            xd, yd, cd = 2 * c + hl, 2 * sq + zh, x % 2
            zd = (z + 4 * (x // 2)) % 8
            same = (xd == x) & (yd == y) & (x // 2 == 0) & (cd == c)
            p_dest.append((device_at(xd, yd, zd, cd), same))
    p_src = []
    away = jnp.where(zh == half, 0, 1)
    for ys in range(4):
        xs, cs = 2 * away + c, x // 2
        zs = (z + 4 * away) % 8
        same = (xs == x) & (ys == y) & (away == 0) & (cs == c)
        p_src.append((device_at(xs, ys, zs, cs), same))
    h_dest = []
    for xd in range(4):
        yd, zd, cd = 2 * zh + c, 4 * half + zl, x // 2
        same = (xd == x) & (yd == y) & (zd == z) & (cd == c)
        h_dest.append((device_at(xd, yd, zd, cd), same))
    h_src = []
    for sq in range(2):
        for hl in range(2):
            xs, ys, zs, cs = 2 * c + hl, 2 * sq + zh, (y // 2) * 4 + zl, y % 2
            same = (xs == x) & (ys == y) & (zs == z) & (cs == c)
            h_src.append((device_at(xs, ys, zs, cs), same))

    bar = pltpu.get_barrier_semaphore()

    def greet(where):
        pl.semaphore_signal(bar, inc=1, device_id=where, device_id_type=MESH)

    def greet_column(d, carry):
        greet(column((j + d) % 16))
        return carry

    lax.fori_loop(1, 16, greet_column, 0)
    for where in (up, down, sib):
        greet(where)
    for where, same in p_src + h_src:

        @pl.when(jnp.logical_not(same))
        def _():
            greet(where)

    expect = 18
    for _, same in p_dest + h_dest:
        expect = expect + jnp.where(same, 0, 1)

    hq = hand_q[...].astype(F32)
    hkv = jnp.concatenate([hand_k[...].astype(F32), hand_v[...].astype(F32)], axis=0)
    for cp in cps_p:
        cp.wait()
    for sq in range(2):
        wide[2 * sq] = in_pk[sq].astype(F32)
        wide[2 * sq + 1] = in_pv[sq].astype(F32)
    for sq in range(2):
        mine = jnp.where(owners[sq] == s, 1.0, 0.0)
        for hl in range(2):
            k = 2 * sq + hl
            stp[k, 0:64, :] = wide[2 * sq, pl.ds(hl, 64, stride=2), :].astype(BF16)
            stp[k, 64:128, :] = wide[2 * sq + 1, pl.ds(hl, 64, stride=2), :].astype(BF16)
            block = jnp.concatenate([hq[:, 8 * hl : 8 * hl + 8, :].reshape(32, 128), hkv], axis=0)
            stp[k, 128:176, :] = (block * mine).astype(BF16)

    pl.semaphore_wait(bar, expect)

    for k, (where, same) in enumerate(p_dest):

        @pl.when(jnp.logical_not(same))
        def _():
            pltpu.make_async_remote_copy(
                stp.at[k], rcp.at[y], p_send.at[k], p_recv, device_id=where, device_id_type=MESH
            ).start()

        @pl.when(same)
        def _():
            pltpu.make_async_copy(stp.at[k], rcp.at[y], p_recv).start()

    for cp in cps_s:
        cp.wait()
    for sq in range(2):
        wide[sq, 0:64, :] = in_k[sq].astype(F32).reshape(64, 128)
        wide[sq, 64:128, :] = in_v[sq].astype(F32).reshape(64, 128)
    for sq in range(2):
        for hh in range(4):
            two = in_q[sq, :, 16 * hh : 16 * hh + 16, :].astype(F32)
            for e in range(2):
                h = 2 * hh + e
                stq[8 * sq + h, 0:64, :] = two[:, 8 * e : 8 * e + 8, :].reshape(64, 128).astype(BF16)
                stq[8 * sq + h, 64:80, :] = jnp.concatenate(
                    [wide[sq, pl.ds(h, 8, stride=8), :], wide[sq, pl.ds(64 + h, 8, stride=8), :]], axis=0
                ).astype(BF16)

    def send_q(d, carry):
        jj = (j + d) % 16
        pltpu.make_async_remote_copy(
            stq.at[jj], rcq.at[j], q_send, q_recv, device_id=column(jj), device_id_type=MESH
        ).start()
        return carry

    lax.fori_loop(1, 16, send_q, 0)
    pltpu.make_async_copy(stq.at[j], rcq.at[j], q_recv).start()

    row = lax.broadcasted_iota(jnp.int32, (1024, 128), 0)
    lane = lax.broadcasted_iota(jnp.int32, (1024, 128), 1)
    dmat[...] = (
        32 * (row // 64) + (row % 64) // 8 - 32 * (lane // 8) - lane % 8
    ).astype(F32)
    top[...] = jnp.full((1024, 128), LOW, F32)
    total[...] = jnp.zeros((1024, 128), F32)
    mixed[...] = jnp.zeros((1024, 128), F32)

    dkpad[...] = jnp.zeros((128, 128), BF16)
    dvpad[...] = jnp.zeros((128, 128), BF16)
    dkpad[0:32, :] = dec_k[...]
    dvpad[0:32, :] = dec_v[...]
    col = lax.broadcasted_iota(jnp.int32, (8, 2048), 1)
    row64 = lax.broadcasted_iota(jnp.int32, (64, 128), 0)
    lane64 = lax.broadcasted_iota(jnp.int32, (64, 128), 1)
    own_ok = (lane64 % 2 == (row64 // 8) % 2) & ((lane64 % 8) // 2 <= row64 // 16)
    for r in range(4):
        cps_k[r].wait()
        qr = dec_q[r]
        sc = dot_t(qr, in_rk[r])
        inside = col // 2 < rlen[r]
        b0 = jnp.where(inside & (col % 2 == 0), 0.0, LOW)
        b1 = jnp.where(inside & (col % 2 == 1), 0.0, LOW)
        both = jnp.concatenate([b0, b1], axis=0)
        sc = sc + jnp.concatenate([both] * 4, axis=0)
        so = jnp.where(own_ok & (lane64 // 8 == r), dot_t(qr, dkpad[...]), LOW)
        mx = jnp.maximum(jnp.max(sc, axis=1, keepdims=True), jnp.max(so, axis=1, keepdims=True))
        ps = jnp.exp2((sc - mx) * SCALE)
        po = jnp.exp2((so - mx) * SCALE)
        den = jnp.sum(ps, axis=1, keepdims=True) + jnp.sum(po, axis=1, keepdims=True)
        cps_v[r].wait()
        num = dot(ps.astype(BF16), in_rv[r]) + dot(po.astype(BF16), dvpad[...])
        resbuf[r] = (num / den).astype(BF16)
    cp_res = pltpu.make_async_copy(resbuf, out_r, sem_out.at[1])
    cp_res.start()

    def recv(ref, sem):
        pltpu.make_async_remote_copy(ref, ref, h_send.at[0], sem, device_id=sib, device_id_type=MESH).wait_recv()

    recv(rcp, p_recv)
    handed = rcp[0, 128:176, :].astype(F32)
    for ys in range(4):
        kv[0, c, 64 * ys : 64 * ys + 64, :] = rcp[ys, 0:64, :]
        kv[0, c, 432 + 64 * ys : 496 + 64 * ys, :] = rcp[ys, 64:128, :]
        if ys:
            handed = handed + rcp[ys, 128:176, :].astype(F32)
    kv[0, c, 384:432, :] = handed.astype(BF16)
    recv(rcq, q_recv)
    new = rcq[:, 64:80, :].astype(F32)
    kv[0, c, 256:384, :] = new[:, 0:8, :].reshape(128, 128).astype(BF16)
    kv[0, c, 688:816, :] = new[:, 8:16, :].reshape(128, 128).astype(BF16)

    parts = (pl.ds(0, 432), pl.ds(432, 384))

    def hop(src, dst, part, where, lane_index):
        pltpu.make_async_remote_copy(
            kv.at[src, c, parts[part]], kv.at[dst, c, parts[part]],
            ring_send.at[lane_index], ring_recv.at[dst, part], device_id=where, device_id_type=MESH,
        ).start()

    def share(slot, part):
        pltpu.make_async_remote_copy(
            kv.at[slot, c, parts[part]], kv.at[slot, c, parts[part]],
            sib_send, sib_recv.at[slot, part], device_id=sib, device_id_type=MESH,
        ).start()

    def arrive(slot, part):
        recv(kv.at[slot, c, parts[part]], ring_recv.at[slot, part])

    def shared(slot):
        for part in (0, 1):
            recv(kv.at[slot, 1 - c, parts[part]], sib_recv.at[slot, part])

    plen_here = plen[seq]
    lane1 = lax.broadcasted_iota(jnp.int32, (1, 128), 1)
    lane_pos = 1024 * (lane1 // 64) + lane1 % 64
    z_of = [z, (z + 7) % 8, (z + 1) % 8, (z + 6) % 8, (z + 2) % 8, (z + 5) % 8, (z + 3) % 8, (z + 4) % 8]

    def prompt_bias(slot, cc):
        zz = z_of[slot]
        off = 256 * (cc + 2 * jnp.where(zz // 4 == half, 0, 1)) + 64 * (zz % 4)
        return [jnp.where(lane_pos + (off + 2048 * e) < plen_here, 0.0, LOW) for e in range(2)]

    def process(slots):
        blocks = [(slot, cc) for slot in slots for cc in range(2)]
        bias = [prompt_bias(slot, cc) for slot, cc in blocks]
        limit = [
            (512 * (2 * (z_of[slot] // 4) + cc - t) + 8 * (z_of[slot] % 4 - zl)).astype(F32)
            for slot, cc in blocks
        ]

        def tile(n):
            rs = pl.ds(n * ROWS, ROWS)
            q = rcq[n * (ROWS // 64) : (n + 1) * (ROWS // 64), 0:64, :].reshape(ROWS, 128)
            keys = jnp.concatenate([kv[slot, cc, 0:384, :] for slot, cc in blocks], axis=0)
            values = jnp.concatenate([kv[slot, cc, 432:816, :] for slot, cc in blocks], axis=0)
            sc = dot_t(q, keys)
            ss = []
            for i in range(len(blocks)):
                ss.append(sc[:, 384 * i : 384 * i + 128] + bias[i][0])
                ss.append(sc[:, 384 * i + 128 : 384 * i + 256] + bias[i][1])
                ss.append(jnp.where(dmat[rs, :] >= limit[i], sc[:, 384 * i + 256 : 384 * i + 384], LOW))
            mx = ss[0]
            for v in ss[1:]:
                mx = jnp.maximum(mx, v)
            old = top[rs, :]
            now = jnp.maximum(old, jnp.max(mx, axis=1, keepdims=True))
            shrink = jnp.exp2((old - now) * SCALE)
            top[rs, :] = now
            ps = [jnp.exp2((v - now) * SCALE) for v in ss]
            su = ps[0]
            for v in ps[1:]:
                su = su + v
            p = jnp.concatenate([v.astype(BF16) for v in ps], axis=1)
            mixed[rs, :] = mixed[rs, :] * shrink + dot(p, values)
            total[rs, :] = total[rs, :] * shrink + su

        for n in range(1024 // ROWS):
            tile(n)

    for part in (0, 1):
        hop(0, 1, part, up, 0)
        hop(0, 2, part, down, 1)
        share(0, part)
    shared(0)
    process([0])
    for a in (1, 2, 3):
        plus, minus = 2 * a - 1, 2 * a
        for part in (0, 1):
            arrive(plus, part)
            if a < 3:
                hop(plus, plus + 2, part, up, 0)
            elif part == 0:
                hop(plus, 7, part, up, 2)
            arrive(minus, part)
            if a < 3:
                hop(minus, minus + 2, part, down, 1)
            elif part == 1:
                hop(minus, 7, part, down, 3)
            share(plus, part)
            share(minus, part)
        shared(plus)
        shared(minus)
        process([plus, minus])
    for part in (0, 1):
        arrive(7, part)
        share(7, part)
    shared(7)
    process([7])

    sto[...] = (mixed[...] / jnp.sum(total[...], axis=1, keepdims=True)).astype(BF16).reshape(16, 64, 128)

    def send_o(d, carry):
        jj = (j + d) % 16
        pltpu.make_async_remote_copy(
            sto.at[jj], rco.at[j], o_send, o_recv, device_id=column(jj), device_id_type=MESH
        ).start()
        return carry

    lax.fori_loop(1, 16, send_o, 0)
    pltpu.make_async_copy(sto.at[j], rco.at[j], o_recv).start()

    hsum = jnp.zeros((48, 128), F32)
    for slot in range(8):
        for cc in range(2):
            hsum = hsum + kv[slot, cc, 384:432, :].astype(F32)
    qh = hsum[0:32, :].astype(BF16)
    dkpad[...] = jnp.zeros((128, 128), BF16)
    dvpad[...] = jnp.zeros((128, 128), BF16)
    zero8 = jnp.zeros((8, 128), F32)
    dkpad[0:16, :] = jnp.concatenate([hsum[32:40, :], zero8], axis=0).astype(BF16)
    dvpad[0:16, :] = jnp.concatenate([hsum[40:48, :], zero8], axis=0).astype(BF16)
    row32 = lax.broadcasted_iota(jnp.int32, (32, 128), 0)
    lane32 = lax.broadcasted_iota(jnp.int32, (32, 128), 1)
    ok = (lane32 < 8) & (lane32 % 2 == x % 2) & (lane32 // 2 <= row32 // 8)
    so = jnp.where(ok, dot_t(qh, dkpad[...]), LOW)
    ss = []
    for slot in range(8):
        for cc in range(2):
            sc = dot_t(qh, kv[slot, cc, 0:384, :])
            bias = prompt_bias(slot, cc)
            ss.append([sc[:, 0:128] + bias[0], sc[:, 128:256] + bias[1], sc[:, 256:384]])
    mx = so
    for three in ss:
        for v in three:
            mx = jnp.maximum(mx, v)
    mx = jnp.max(mx, axis=1, keepdims=True)
    po = jnp.exp2((so - mx) * SCALE)
    su = po
    num = dot(po.astype(BF16), dvpad[...])
    for i, three in enumerate(ss):
        ps = [jnp.exp2((v - mx) * SCALE) for v in three]
        su = su + ps[0] + ps[1] + ps[2]
        p = jnp.concatenate([v.astype(BF16) for v in ps], axis=1)
        num = num + dot(p, kv[i // 2, i % 2, 432:816, :])
    sth[...] = (num / jnp.sum(su, axis=1, keepdims=True)).astype(BF16)
    slot_h = seq * 2 + x % 2
    for k, (where, same) in enumerate(h_dest):

        @pl.when(jnp.logical_not(same))
        def _():
            pltpu.make_async_remote_copy(
                sth, rch.at[slot_h], h_send.at[k], h_recv, device_id=where, device_id_type=MESH
            ).start()

        @pl.when(same)
        def _():
            pltpu.make_async_copy(sth, rch.at[slot_h], h_recv).start()

    recv(rco, o_recv)
    for sq in range(2):
        for hh in range(4):
            a = rco[8 * sq + 2 * hh].astype(F32).reshape(8, 8, 128)
            b = rco[8 * sq + 2 * hh + 1].astype(F32).reshape(8, 8, 128)
            outbuf[sq, :, 16 * hh : 16 * hh + 16, :] = jnp.concatenate([a, b], axis=1).astype(BF16)
    cp_out = pltpu.make_async_copy(outbuf, out_p, sem_out.at[0])
    cp_out.start()
    recv(rch, h_recv)
    heads = []
    for hl in range(2):
        acc = jnp.zeros((32, 128), F32)
        for sq in range(2):
            mine = jnp.where(owners[sq] == s, 1.0, 0.0)
            acc = acc + rch[2 * sq + hl].astype(F32) * mine
        heads.append(acc.reshape(4, 8, 128))
    out_h[...] = jnp.concatenate(heads, axis=1).astype(BF16)

    def sent(ref, sem):
        pltpu.make_async_remote_copy(ref, ref, sem, h_recv, device_id=sib, device_id_type=MESH).wait_send()

    for k, (_, same) in enumerate(p_dest):

        @pl.when(jnp.logical_not(same))
        def _():
            sent(stp.at[k], p_send.at[k])

    for k, (_, same) in enumerate(h_dest):

        @pl.when(jnp.logical_not(same))
        def _():
            sent(sth, h_send.at[k])

    sent(stq.at[pl.ds(0, 15)], q_send)
    sent(sto.at[pl.ds(0, 15)], o_send)
    sent(kv.at[pl.ds(0, 3), 0], ring_send.at[0])
    sent(kv.at[pl.ds(0, 3), 0], ring_send.at[1])
    sent(kv.at[0, 0, parts[0]], ring_send.at[2])
    sent(kv.at[0, 0, parts[1]], ring_send.at[3])
    sent(kv.at[pl.ds(0, 8), 0], sib_send)
    cp_out.wait()
    cp_res.wait()


def on_device(
    prompt_lengths, owners, span_q, span_k, span_v, prompt_keys, prompt_values, res_lengths,
    res_keys, res_values, dec_q, dec_k, dec_v, hand_q, hand_k, hand_v,
):
    smem = pl.BlockSpec(memory_space=pltpu.SMEM)
    hbm = pl.BlockSpec(memory_space=pl.ANY)
    vmem = pl.BlockSpec(memory_space=pltpu.VMEM)
    dma = pltpu.SemaphoreType.DMA
    out = pl.pallas_call(
        kernel,
        out_shape=(
            jax.ShapeDtypeStruct((2, 8, 64, 128), BF16),
            jax.ShapeDtypeStruct((4, 64, 128), BF16),
            jax.ShapeDtypeStruct((4, 16, 128), BF16),
        ),
        in_specs=[smem] * 3 + [hbm] * 7 + [vmem] * 6,
        out_specs=(hbm, hbm, vmem),
        scratch_shapes=[
            pltpu.VMEM((2, 8, 64, 128), BF16),
            pltpu.VMEM((2, 8, 8, 128), BF16),
            pltpu.VMEM((2, 8, 8, 128), BF16),
            pltpu.VMEM((2, 128, 128), BF16),
            pltpu.VMEM((2, 128, 128), BF16),
            pltpu.VMEM((4, 2048, 128), BF16),
            pltpu.VMEM((4, 2048, 128), BF16),
            pltpu.VMEM((4, 128, 128), F32),
            pltpu.VMEM((16, 80, 128), BF16),
            pltpu.VMEM((16, 80, 128), BF16),
            pltpu.VMEM((4, 176, 128), BF16),
            pltpu.VMEM((4, 176, 128), BF16),
            pltpu.VMEM((8, 2, 816, 128), BF16),
            pltpu.VMEM((1024, 128), F32),
            pltpu.VMEM((1024, 128), F32),
            pltpu.VMEM((1024, 128), F32),
            pltpu.VMEM((1024, 128), F32),
            pltpu.VMEM((16, 64, 128), BF16),
            pltpu.VMEM((16, 64, 128), BF16),
            pltpu.VMEM((32, 128), BF16),
            pltpu.VMEM((4, 32, 128), BF16),
            pltpu.VMEM((2, 8, 64, 128), BF16),
            pltpu.VMEM((4, 64, 128), BF16),
            pltpu.VMEM((128, 128), BF16),
            pltpu.VMEM((128, 128), BF16),
            dma((5,)), dma((4,)), dma((4,)), dma((2,)),
            dma, dma, dma((4,)), dma, dma((4,)), dma((8, 2)), dma, dma((8, 2)),
            dma, dma, dma((4,)), dma,
        ],
        compiler_params=pltpu.CompilerParams(
            collective_id=0, has_side_effects=True, vmem_limit_bytes=52 << 20
        ),
        name="spanned",
    )(
        prompt_lengths, owners, res_lengths, span_q, span_k, span_v,
        prompt_keys.reshape(2, 128, 128), prompt_values.reshape(2, 128, 128),
        res_keys.reshape(4, 2048, 128), res_values.reshape(4, 2048, 128),
        dec_q.reshape(4, 64, 128), dec_k.reshape(32, 128), dec_v.reshape(32, 128),
        hand_q.reshape(4, 16, 128), hand_k.reshape(8, 128), hand_v.reshape(8, 128),
    )
    prefill_out, res_out, hand_out = out
    return (prefill_out, res_out.reshape(4, 4, 16, 128), hand_out.reshape(1, 4, 16, 128))


def solution(mesh):
    cache = P("section", None, "tensor", None)
    span = P(None, ("tensor", "section"), None, None)
    prompt = P(None, "section", "tensor", None)
    return jax.shard_map(
        on_device,
        mesh=mesh,
        in_specs=(P(), P(), span, span, span, prompt, prompt, P("section")) + (cache,) * 8,
        out_specs=(span, cache, cache),
        check_vma=False,
    )
```

```python
import jax
import jax.numpy as jnp
from jax import lax
from jax.experimental import pallas as pl
from jax.experimental.pallas import tpu as pltpu
from jax.sharding import PartitionSpec as P

MESH = pl.DeviceIdType.MESH
F32 = jnp.float32
BF16 = jnp.bfloat16
SCALE = 128 ** -0.5 * 1.4426950408889634
LOW = -1e30
ROWS = 512


def device_at(x, y, z, c):
    return ((z // 4) * 2 + c, y * 16 + x * 4 + z % 4)


def dot_t(a, b):
    return lax.dot_general(a, b, (((1,), (1,)), ((), ())), preferred_element_type=F32)


def dot(a, b):
    return jnp.dot(a, b, preferred_element_type=F32)


def kernel(
    plen_h, owners_h, rlen_h, span_q, span_k, span_v, prompt_k, prompt_v, res_k, res_v,
    dec_q_h, dec_k_h, dec_v_h, hand_q_h, hand_k_h, hand_v_h,
    rco, out_r, out_h,
    in_q, in_k, in_v, in_pk, in_pv, in_rk, in_rv,
    plen, owners, rlen, dec_q, dec_k, dec_v, hand_q, hand_k, hand_v, hbuf,
    wide, stn, rcn, stq, rcq, stp, rcp, kv, top, total, mixed, dmat, sto, sth, rch,
    resbuf, dkpad, dvpad,
    sem_in, sem_rk, sem_rv, sem_out,
    n_send, n_recv, q_send, q_recv, p_send, p_recv, ring_send, ring_recv, sib_send, sib_recv,
    o_send, o_recv, h_send, h_recv,
):
    t = lax.axis_index("tensor")
    s = lax.axis_index("section")
    zh, c = t // 2, t % 2
    x, y, zl = (s // 4) % 4, s // 16, s % 4
    z = zh * 4 + zl
    j = s // 4
    seq, half = y // 2, y % 2

    def copy_in(a, b, sem):
        cp = pltpu.make_async_copy(a, b, sem)
        cp.start()
        return cp

    def column(jj):
        return device_at(jj % 4, jj // 4, z, c)

    up = device_at(x, y, (z + 1) % 8, c)
    down = device_at(x, y, (z + 7) % 8, c)
    sib = device_at(x, y, z, 1 - c)

    p_dest = []
    for sq in range(2):
        for hl in range(2):
            xd, yd, cd = 2 * c + hl, 2 * sq + zh, x % 2
            cross = x // 2 != sq
            zd = jnp.where(cross, 7 - z, z)
            same = (xd == x) & (yd == y) & jnp.logical_not(cross) & (cd == c)
            p_dest.append((device_at(xd, yd, zd, cd), same))
    p_src = []
    away = zh != half
    for ys in range(4):
        xs, cs = 2 * jnp.where(away, 1 - seq, seq) + c, x // 2
        zs = jnp.where(away, 7 - z, z)
        same = (xs == x) & (ys == y) & jnp.logical_not(away) & (cs == c)
        p_src.append((device_at(xs, ys, zs, cs), same))
    member = zh == half
    h_dest = []
    for yd in range(2):
        for xd in range(4):
            yy, cd = 2 * yd + c, x // 2
            same = (xd == x) & (yy == y) & (cd == c)
            h_dest.append((device_at(xd, yy, z, cd), same, member & jnp.logical_not(same)))
    h_src = []
    for sq in range(2):
        for hl in range(2):
            xs, ys, cs = 2 * c + hl, 2 * sq + zh, y % 2
            same = (xs == x) & (ys == y) & (cs == c)
            h_src.append((device_at(xs, ys, z, cs), same))

    bar = pltpu.get_barrier_semaphore()

    def greet(where):
        pl.semaphore_signal(bar, inc=1, device_id=where, device_id_type=MESH)

    def greet_column(d, carry):
        greet(column((j + d) % 16))
        return carry

    for where, same in p_src + h_src:

        @pl.when(jnp.logical_not(same))
        def _():
            greet(where)

    lax.fori_loop(1, 16, greet_column, 0)
    for where in (up, down, sib):
        greet(where)
    cps_p = [copy_in(prompt_k, in_pk, sem_in.at[0]), copy_in(prompt_v, in_pv, sem_in.at[1])]
    cps_h = [
        copy_in(a, b, sem_in.at[5 + i])
        for i, (a, b) in enumerate(
            [(owners_h, owners), (hand_q_h, hand_q), (hand_k_h, hand_k), (hand_v_h, hand_v)]
        )
    ]
    cps_s = [
        copy_in(span_k, in_k, sem_in.at[2]),
        copy_in(span_v, in_v, sem_in.at[3]),
        copy_in(span_q, in_q, sem_in.at[4]),
    ]
    cps_d = [
        copy_in(a, b, sem_in.at[9 + i])
        for i, (a, b) in enumerate(
            [(plen_h, plen), (rlen_h, rlen), (dec_q_h, dec_q), (dec_k_h, dec_k), (dec_v_h, dec_v)]
        )
    ]
    cps_k = [copy_in(res_k.at[r], in_rk.at[r], sem_rk.at[r]) for r in range(4)]
    cps_v = [copy_in(res_v.at[r], in_rv.at[r], sem_rv.at[r]) for r in range(4)]

    expect = 18
    for _, same in p_dest:
        expect = expect + jnp.where(same, 0, 1)
    for _, _, go in h_dest:
        expect = expect + jnp.where(go, 1, 0)

    for cp in cps_h:
        cp.wait()
    hq = hand_q[...].astype(F32)
    hkv = jnp.concatenate([hand_k[...].astype(F32), hand_v[...].astype(F32)], axis=0)
    for cp in cps_p:
        cp.wait()
    for sq in range(2):
        wide[2 * sq] = in_pk[sq].astype(F32)
        wide[2 * sq + 1] = in_pv[sq].astype(F32)
    for sq in range(2):
        mine = jnp.where(owners[sq] == s, 1.0, 0.0)
        for hl in range(2):
            k = 2 * sq + hl
            stp[k, 0:64, :] = wide[2 * sq, pl.ds(hl, 64, stride=2), :].astype(BF16)
            stp[k, 64:128, :] = wide[2 * sq + 1, pl.ds(hl, 64, stride=2), :].astype(BF16)
            block = jnp.concatenate([hq[:, 8 * hl : 8 * hl + 8, :].reshape(32, 128), hkv], axis=0)
            stp[k, 128:176, :] = (block * mine).astype(BF16)

    pl.semaphore_wait(bar, expect)

    for k, (where, same) in enumerate(p_dest):

        @pl.when(jnp.logical_not(same))
        def _():
            pltpu.make_async_remote_copy(
                stp.at[k], rcp.at[y], p_send.at[k], p_recv, device_id=where, device_id_type=MESH
            ).start()

        @pl.when(same)
        def _():
            pltpu.make_async_copy(stp.at[k], rcp.at[y], p_recv).start()

    for cp in cps_s:
        cp.wait()
    for sq in range(2):
        wide[sq, 0:64, :] = in_k[sq].astype(F32).reshape(64, 128)
        wide[sq, 64:128, :] = in_v[sq].astype(F32).reshape(64, 128)
    for sq in range(2):
        for h in range(8):
            stn[8 * sq + h] = jnp.concatenate(
                [wide[sq, pl.ds(h, 8, stride=8), :], wide[sq, pl.ds(64 + h, 8, stride=8), :]], axis=0
            ).astype(BF16)

    def send_n(d, carry):
        jj = (j + d) % 16
        pltpu.make_async_remote_copy(
            stn.at[jj], rcn.at[j], n_send, n_recv, device_id=column(jj), device_id_type=MESH
        ).start()
        return carry

    lax.fori_loop(1, 16, send_n, 0)
    pltpu.make_async_copy(stn.at[j], rcn.at[j], n_recv).start()

    for sq in range(2):
        for hh in range(4):
            two = in_q[sq, :, 16 * hh : 16 * hh + 16, :].astype(F32)
            for e in range(2):
                h = 2 * hh + e
                stq[8 * sq + h] = two[:, 8 * e : 8 * e + 8, :].reshape(64, 128).astype(BF16)

    def send_q(d, carry):
        jj = (j + d) % 16
        pltpu.make_async_remote_copy(
            stq.at[jj], rcq.at[j], q_send, q_recv, device_id=column(jj), device_id_type=MESH
        ).start()
        return carry

    lax.fori_loop(1, 16, send_q, 0)
    pltpu.make_async_copy(stq.at[j], rcq.at[j], q_recv).start()

    row = lax.broadcasted_iota(jnp.int32, (1024, 128), 0)
    lane = lax.broadcasted_iota(jnp.int32, (1024, 128), 1)
    dmat[...] = (
        32 * (row // 64) + (row % 64) // 8 - 32 * (lane // 8) - lane % 8
    ).astype(F32)
    top[...] = jnp.full((1024, 128), LOW, F32)
    total[...] = jnp.zeros((1024, 128), F32)
    mixed[...] = jnp.zeros((1024, 128), F32)

    for cp in cps_d:
        cp.wait()
    dkpad[...] = jnp.zeros((128, 128), BF16)
    dvpad[...] = jnp.zeros((128, 128), BF16)
    dkpad[0:32, :] = dec_k[...]
    dvpad[0:32, :] = dec_v[...]
    col = lax.broadcasted_iota(jnp.int32, (8, 2048), 1)
    row64 = lax.broadcasted_iota(jnp.int32, (64, 128), 0)
    lane64 = lax.broadcasted_iota(jnp.int32, (64, 128), 1)
    own_ok = (lane64 % 2 == (row64 // 8) % 2) & ((lane64 % 8) // 2 <= row64 // 16)
    for r in range(4):
        cps_k[r].wait()
        qr = dec_q[r]
        sc = dot_t(qr, in_rk[r])
        inside = col // 2 < rlen[r]
        b0 = jnp.where(inside & (col % 2 == 0), 0.0, LOW)
        b1 = jnp.where(inside & (col % 2 == 1), 0.0, LOW)
        both = jnp.concatenate([b0, b1], axis=0)
        sc = sc + jnp.concatenate([both] * 4, axis=0)
        so = jnp.where(own_ok & (lane64 // 8 == r), dot_t(qr, dkpad[...]), LOW)
        mx = jnp.maximum(jnp.max(sc, axis=1, keepdims=True), jnp.max(so, axis=1, keepdims=True))
        ps = jnp.exp2((sc - mx) * SCALE)
        po = jnp.exp2((so - mx) * SCALE)
        den = jnp.sum(ps, axis=1, keepdims=True) + jnp.sum(po, axis=1, keepdims=True)
        cps_v[r].wait()
        num = dot(ps.astype(BF16), in_rv[r]) + dot(po.astype(BF16), dvpad[...])
        resbuf[r] = (num / den).astype(BF16)
    cp_res = pltpu.make_async_copy(resbuf, out_r, sem_out.at[0])
    cp_res.start()

    def recv(ref, sem):
        pltpu.make_async_remote_copy(ref, ref, h_send.at[0], sem, device_id=sib, device_id_type=MESH).wait_recv()

    parts = (pl.ds(0, 416), pl.ds(416, 400))

    def hop(src, dst, part, where, lane_index):
        pltpu.make_async_remote_copy(
            kv.at[src, c, parts[part]], kv.at[dst, c, parts[part]],
            ring_send.at[lane_index], ring_recv.at[dst, part], device_id=where, device_id_type=MESH,
        ).start()

    def share(slot, part):
        pltpu.make_async_remote_copy(
            kv.at[slot, c, parts[part]], kv.at[slot, c, parts[part]],
            sib_send, sib_recv.at[slot, part], device_id=sib, device_id_type=MESH,
        ).start()

    def arrive(slot, part):
        recv(kv.at[slot, c, parts[part]], ring_recv.at[slot, part])

    def shared(slot):
        for part in (0, 1):
            recv(kv.at[slot, 1 - c, parts[part]], sib_recv.at[slot, part])

    recv(rcp, p_recv)
    handed = rcp[0, 128:176, :].astype(F32)
    for ys in range(4):
        kv[0, c, 64 * ys : 64 * ys + 64, :] = rcp[ys, 0:64, :]
        kv[0, c, 256 + 64 * ys : 320 + 64 * ys, :] = rcp[ys, 64:128, :]
        if ys:
            handed = handed + rcp[ys, 128:176, :].astype(F32)
    kv[0, c, 512:560, :] = handed.astype(BF16)
    hop(0, 1, 0, up, 0)
    hop(0, 2, 0, down, 1)
    share(0, 0)
    recv(rcn, n_recv)
    new = rcn[...].astype(F32)
    kv[0, c, 560:688, :] = new[:, 0:8, :].reshape(128, 128).astype(BF16)
    kv[0, c, 688:816, :] = new[:, 8:16, :].reshape(128, 128).astype(BF16)
    hop(0, 1, 1, up, 0)
    hop(0, 2, 1, down, 1)
    share(0, 1)

    plen_here = plen[seq]
    lane1 = lax.broadcasted_iota(jnp.int32, (1, 128), 1)
    lane_pos = 1024 * (lane1 // 64) + lane1 % 64
    z_of = [z, (z + 7) % 8, (z + 1) % 8, (z + 6) % 8, (z + 2) % 8, (z + 5) % 8, (z + 3) % 8, (z + 4) % 8]

    def prompt_bias(slot, cc):
        zz = z_of[slot]
        near = 256 * (cc + 2 * seq) + 64 * (zz % 4)
        far = 256 * (cc + 2 * (1 - seq)) + 64 * (3 - zz % 4)
        off = jnp.where(zz // 4 == half, near, far)
        return [jnp.where(lane_pos + (off + 2048 * e) < plen_here, 0.0, LOW) for e in range(2)]

    def process(blocks, after=None):
        rows = ROWS if after is not None else 1024
        bias = [prompt_bias(slot, cc) for slot, cc in blocks]
        limit = [
            (512 * (2 * (z_of[slot] // 4) + cc - t) + 8 * (z_of[slot] % 4 - zl)).astype(F32)
            for slot, cc in blocks
        ]

        def tile(n):
            rs = pl.ds(n * rows, rows)
            q = rcq[n * (rows // 64) : (n + 1) * (rows // 64), :, :].reshape(rows, 128)
            keys = jnp.concatenate(
                [kv[slot, cc, part, :] for slot, cc in blocks for part in (slice(0, 256), slice(560, 688))], axis=0
            )
            values = jnp.concatenate(
                [kv[slot, cc, part, :] for slot, cc in blocks for part in (slice(256, 512), slice(688, 816))], axis=0
            )
            sc = dot_t(q, keys)
            ss = []
            for i in range(len(blocks)):
                ss.append(sc[:, 384 * i : 384 * i + 128] + bias[i][0])
                ss.append(sc[:, 384 * i + 128 : 384 * i + 256] + bias[i][1])
                ss.append(jnp.where(dmat[rs, :] >= limit[i], sc[:, 384 * i + 256 : 384 * i + 384], LOW))
            mx = ss[0]
            for v in ss[1:]:
                mx = jnp.maximum(mx, v)
            old = top[rs, :]
            now = jnp.maximum(old, jnp.max(mx, axis=1, keepdims=True))
            shrink = jnp.exp2((old - now) * SCALE)
            top[rs, :] = now
            ps = [jnp.exp2((v - now) * SCALE) for v in ss]
            su = ps[0]
            for v in ps[1:]:
                su = su + v
            p = jnp.concatenate([v.astype(BF16) for v in ps], axis=1)
            mixed[rs, :] = mixed[rs, :] * shrink + dot(p, values)
            total[rs, :] = total[rs, :] * shrink + su

        for n in range(1024 // rows):
            tile(n)
            if after is not None:
                after(n)

    def send_o(n):
        rs = pl.ds(n * ROWS, ROWS)
        count = ROWS // 64
        part = mixed[rs, :] / jnp.sum(total[rs, :], axis=1, keepdims=True)
        sto[n * count : (n + 1) * count] = part.astype(BF16).reshape(count, 64, 128)

        def one(d, carry):
            jj = n * count + (j + d) % count

            @pl.when(jj != j)
            def _():
                pltpu.make_async_remote_copy(
                    sto.at[jj], rco.at[j], o_send, o_recv, device_id=column(jj), device_id_type=MESH
                ).start()

            @pl.when(jj == j)
            def _():
                pltpu.make_async_copy(sto.at[jj], rco.at[j], o_recv).start()

            return carry

        lax.fori_loop(0, count, one, 0)

    def theirs(slots):
        for slot in slots:
            shared(slot)
        process([(slot, 1 - c) for slot in slots])

    recv(rcq, q_recv)
    process([(0, c)])
    for a in (1, 2, 3):
        plus, minus = 2 * a - 1, 2 * a
        for part in (0, 1):
            arrive(plus, part)
            if a < 3:
                hop(plus, plus + 2, part, up, 0)
            elif part == 0:
                hop(plus, 7, part, up, 2)
            arrive(minus, part)
            if a < 3:
                hop(minus, minus + 2, part, down, 1)
            elif part == 1:
                hop(minus, 7, part, down, 3)
            share(plus, part)
            share(minus, part)
            if part == 0:
                theirs([0] if a == 1 else [plus - 2, minus - 2])
        process([(plus, c), (minus, c)])
    arrive(7, 0)
    share(7, 0)
    theirs([5, 6])
    arrive(7, 1)
    share(7, 1)
    process([(7, c)])
    shared(7)
    process([(7, 1 - c)], send_o)

    hsum = jnp.zeros((48, 128), F32)
    for slot in range(8):
        for cc in range(2):
            hsum = hsum + kv[slot, cc, 512:560, :].astype(F32)
    qh = hsum[0:32, :].astype(BF16)
    dkpad[...] = jnp.zeros((128, 128), BF16)
    dvpad[...] = jnp.zeros((128, 128), BF16)
    zero8 = jnp.zeros((8, 128), F32)
    dkpad[0:16, :] = jnp.concatenate([hsum[32:40, :], zero8], axis=0).astype(BF16)
    dvpad[0:16, :] = jnp.concatenate([hsum[40:48, :], zero8], axis=0).astype(BF16)
    row32 = lax.broadcasted_iota(jnp.int32, (32, 128), 0)
    lane32 = lax.broadcasted_iota(jnp.int32, (32, 128), 1)
    ok = (lane32 < 8) & (lane32 % 2 == x % 2) & (lane32 // 2 <= row32 // 8)
    so = jnp.where(ok, dot_t(qh, dkpad[...]), LOW)
    ss = []
    for slot in range(8):
        for cc in range(2):
            sc = dot_t(qh, jnp.concatenate([kv[slot, cc, 0:256, :], kv[slot, cc, 560:688, :]], axis=0))
            bias = prompt_bias(slot, cc)
            ss.append([sc[:, 0:128] + bias[0], sc[:, 128:256] + bias[1], sc[:, 256:384]])
    mx = so
    for three in ss:
        for v in three:
            mx = jnp.maximum(mx, v)
    mx = jnp.max(mx, axis=1, keepdims=True)
    po = jnp.exp2((so - mx) * SCALE)
    su = po
    num = dot(po.astype(BF16), dvpad[...])
    for i, three in enumerate(ss):
        ps = [jnp.exp2((v - mx) * SCALE) for v in three]
        su = su + ps[0] + ps[1] + ps[2]
        p = jnp.concatenate([v.astype(BF16) for v in ps], axis=1)
        num = num + dot(
            p, jnp.concatenate([kv[i // 2, i % 2, 256:512, :], kv[i // 2, i % 2, 688:816, :]], axis=0)
        )
    sth[...] = (num / jnp.sum(su, axis=1, keepdims=True)).astype(BF16)
    slot_h = seq * 2 + x % 2
    for k, (where, same, go) in enumerate(h_dest):

        @pl.when(go)
        def _():
            pltpu.make_async_remote_copy(
                sth, rch.at[slot_h], h_send.at[k], h_recv, device_id=where, device_id_type=MESH
            ).start()

        @pl.when(member & same)
        def _():
            pltpu.make_async_copy(sth, rch.at[slot_h], h_recv).start()

    recv(rch, h_recv)
    heads = []
    for hl in range(2):
        acc = jnp.zeros((32, 128), F32)
        for sq in range(2):
            mine = jnp.where(owners[sq] == s, 1.0, 0.0)
            acc = acc + rch[2 * sq + hl].astype(F32) * mine
        heads.append(acc.reshape(4, 8, 128))
    hbuf[...] = jnp.concatenate(heads, axis=1).astype(BF16)
    cp_hand = pltpu.make_async_copy(hbuf, out_h, sem_out.at[1])
    cp_hand.start()

    recv(rco, o_recv)

    def sent(ref, sem):
        pltpu.make_async_remote_copy(ref, ref, sem, h_recv, device_id=sib, device_id_type=MESH).wait_send()

    for k, (_, same) in enumerate(p_dest):

        @pl.when(jnp.logical_not(same))
        def _():
            sent(stp.at[k], p_send.at[k])

    for k, (_, same, go) in enumerate(h_dest):

        @pl.when(go)
        def _():
            sent(sth, h_send.at[k])

    sent(stn.at[pl.ds(0, 15)], n_send)
    sent(stq.at[pl.ds(0, 15)], q_send)
    sent(sto.at[pl.ds(0, 15)], o_send)
    sent(kv.at[pl.ds(0, 3), 0], ring_send.at[0])
    sent(kv.at[pl.ds(0, 3), 0], ring_send.at[1])
    sent(kv.at[0, 0, parts[0]], ring_send.at[2])
    sent(kv.at[0, 0, parts[1]], ring_send.at[3])
    sent(kv.at[pl.ds(0, 8), 0], sib_send)
    cp_res.wait()
    cp_hand.wait()


def place(got, res, hand, out_p, out_r, out_h, pieces, whole, sem_in, sem_out):
    cp_r = pltpu.make_async_copy(res, out_r, sem_out.at[2])
    cp_h = pltpu.make_async_copy(hand, out_h, sem_out.at[3])
    loads = [
        pltpu.make_async_copy(got.at[pl.ds(8 * sq, 8)], pieces.at[pl.ds(8 * sq, 8)], sem_in.at[sq])
        for sq in range(2)
    ]
    for cp in loads:
        cp.start()
    cp_r.start()
    cp_h.start()
    stores = []
    for sq in range(2):
        loads[sq].wait()
        for hh in range(4):
            a = pieces[8 * sq + 2 * hh].astype(F32).reshape(8, 8, 128)
            b = pieces[8 * sq + 2 * hh + 1].astype(F32).reshape(8, 8, 128)
            whole[sq, :, 16 * hh : 16 * hh + 16, :] = jnp.concatenate([a, b], axis=1).astype(BF16)
        cp = pltpu.make_async_copy(whole.at[sq], out_p.at[sq], sem_out.at[sq])
        cp.start()
        stores.append(cp)
    for cp in stores:
        cp.wait()
    cp_r.wait()
    cp_h.wait()


def on_device(
    prompt_lengths, owners, span_q, span_k, span_v, prompt_keys, prompt_values, res_lengths,
    res_keys, res_values, dec_q, dec_k, dec_v, hand_q, hand_k, hand_v,
):
    hbm = pl.BlockSpec(memory_space=pltpu.HBM)
    dma = pltpu.SemaphoreType.DMA
    out = pl.pallas_call(
        kernel,
        out_shape=(
            jax.ShapeDtypeStruct((16, 64, 128), BF16),
            jax.ShapeDtypeStruct((4, 64, 128), BF16),
            jax.ShapeDtypeStruct((4, 16, 128), BF16),
        ),
        in_specs=[hbm] * 16,
        out_specs=(hbm, hbm, hbm),
        scratch_shapes=[
            pltpu.VMEM((2, 8, 64, 128), BF16),
            pltpu.VMEM((2, 8, 8, 128), BF16),
            pltpu.VMEM((2, 8, 8, 128), BF16),
            pltpu.VMEM((2, 128, 128), BF16),
            pltpu.VMEM((2, 128, 128), BF16),
            pltpu.VMEM((4, 2048, 128), BF16),
            pltpu.VMEM((4, 2048, 128), BF16),
            pltpu.SMEM((2,), jnp.int32),
            pltpu.SMEM((2,), jnp.int32),
            pltpu.SMEM((4,), jnp.int32),
            pltpu.VMEM((4, 64, 128), BF16),
            pltpu.VMEM((32, 128), BF16),
            pltpu.VMEM((32, 128), BF16),
            pltpu.VMEM((4, 16, 128), BF16),
            pltpu.VMEM((8, 128), BF16),
            pltpu.VMEM((8, 128), BF16),
            pltpu.VMEM((4, 16, 128), BF16),
            pltpu.VMEM((4, 128, 128), F32),
            pltpu.VMEM((16, 16, 128), BF16),
            pltpu.VMEM((16, 16, 128), BF16),
            pltpu.VMEM((16, 64, 128), BF16),
            pltpu.VMEM((16, 64, 128), BF16),
            pltpu.VMEM((4, 176, 128), BF16),
            pltpu.VMEM((4, 176, 128), BF16),
            pltpu.VMEM((8, 2, 816, 128), BF16),
            pltpu.VMEM((1024, 128), F32),
            pltpu.VMEM((1024, 128), F32),
            pltpu.VMEM((1024, 128), F32),
            pltpu.VMEM((1024, 128), F32),
            pltpu.VMEM((16, 64, 128), BF16),
            pltpu.VMEM((32, 128), BF16),
            pltpu.VMEM((4, 32, 128), BF16),
            pltpu.VMEM((4, 64, 128), BF16),
            pltpu.VMEM((128, 128), BF16),
            pltpu.VMEM((128, 128), BF16),
            dma((14,)), dma((4,)), dma((4,)), dma((2,)),
            dma, dma, dma, dma, dma((4,)), dma, dma((4,)), dma((8, 2)), dma, dma((8, 2)),
            dma, dma, dma((8,)), dma,
        ],
        compiler_params=pltpu.CompilerParams(
            collective_id=0, has_side_effects=True, vmem_limit_bytes=64 << 20
        ),
        name="spanned",
    )(
        prompt_lengths, owners, res_lengths, span_q, span_k, span_v,
        prompt_keys.reshape(2, 128, 128), prompt_values.reshape(2, 128, 128),
        res_keys.reshape(4, 2048, 128), res_values.reshape(4, 2048, 128),
        dec_q.reshape(4, 64, 128), dec_k.reshape(32, 128), dec_v.reshape(32, 128),
        hand_q.reshape(4, 16, 128), hand_k.reshape(8, 128), hand_v.reshape(8, 128),
    )
    any_space = pl.BlockSpec(memory_space=pl.ANY)
    prefill_out, res_out, hand_out = pl.pallas_call(
        place,
        out_shape=(
            jax.ShapeDtypeStruct((2, 8, 64, 128), BF16),
            jax.ShapeDtypeStruct((4, 64, 128), BF16),
            jax.ShapeDtypeStruct((4, 16, 128), BF16),
        ),
        in_specs=[any_space] * 3,
        out_specs=(any_space,) * 3,
        scratch_shapes=[
            pltpu.VMEM((16, 64, 128), BF16), pltpu.VMEM((2, 8, 64, 128), BF16), dma((2,)), dma((4,)),
        ],
        compiler_params=pltpu.CompilerParams(vmem_limit_bytes=64 << 20),
        name="place",
    )(*out)
    return (prefill_out, res_out.reshape(4, 4, 16, 128), hand_out.reshape(1, 4, 16, 128))


def solution(mesh):
    cache = P("section", None, "tensor", None)
    span = P(None, ("tensor", "section"), None, None)
    prompt = P(None, "section", "tensor", None)
    return jax.shard_map(
        on_device,
        mesh=mesh,
        in_specs=(P(), P(), span, span, span, prompt, prompt, P("section")) + (cache,) * 8,
        out_specs=(span, cache, cache),
        check_vma=False,
    )
```

```python
import jax
import jax.numpy as jnp
from jax import lax
from jax.experimental import pallas as pl
from jax.experimental.pallas import tpu as pltpu
from jax.sharding import PartitionSpec as P

MESH = pl.DeviceIdType.MESH
F32 = jnp.float32
BF16 = jnp.bfloat16
SCALE = 128 ** -0.5 * 1.4426950408889634
LOW = -1e30
ROWS = 512


def device_at(x, y, z, c):
    return ((z // 4) * 2 + c, y * 16 + x * 4 + z % 4)


def dot_t(a, b):
    return lax.dot_general(a, b, (((1,), (1,)), ((), ())), preferred_element_type=F32)


def dot(a, b):
    return jnp.dot(a, b, preferred_element_type=F32)


def kernel(
    plen_h, owners_h, rlen_h, span_q, span_k, span_v, prompt_k, prompt_v, res_k, res_v,
    dec_q_h, dec_k_h, dec_v_h, hand_q_h, hand_k_h, hand_v_h,
    rco, out_r, out_h,
    in_q, in_k, in_v, in_pk, in_pv, in_rk, in_rv,
    plen, owners, rlen, dec_q, dec_k, dec_v, hand_q, hand_k, hand_v, hbuf,
    wide, stn, rcn, stq, rcq, stp, rcp, kv, top, total, mixed, dmat, sto, sth, rch,
    resbuf, dkpad, dvpad,
    sem_in, sem_rk, sem_rv, sem_out,
    n_send, n_recv, q_send, q_recv, p_send, p_recv, ring_send, ring_recv, sib_send, sib_recv,
    o_send, o_recv, h_send, h_recv,
):
    t = lax.axis_index("tensor")
    s = lax.axis_index("section")
    zh, c = t // 2, t % 2
    x, y, zl = (s // 4) % 4, s // 16, s % 4
    z = zh * 4 + zl
    j = s // 4
    seq, half = y // 2, y % 2

    def copy_in(a, b, sem):
        cp = pltpu.make_async_copy(a, b, sem)
        cp.start()
        return cp

    def column(jj):
        return device_at(jj % 4, jj // 4, z, c)

    up = device_at(x, y, (z + 1) % 8, c)
    down = device_at(x, y, (z + 7) % 8, c)
    sib = device_at(x, y, z, 1 - c)

    p_dest = []
    for sq in range(2):
        for hl in range(2):
            xd, yd, cd = 2 * c + hl, 2 * sq + zh, x % 2
            cross = x // 2 != sq
            zd = jnp.where(cross, 7 - z, z)
            same = (xd == x) & (yd == y) & jnp.logical_not(cross) & (cd == c)
            p_dest.append((device_at(xd, yd, zd, cd), same))
    p_src = []
    away = zh != half
    for ys in range(4):
        xs, cs = 2 * jnp.where(away, 1 - seq, seq) + c, x // 2
        zs = jnp.where(away, 7 - z, z)
        same = (xs == x) & (ys == y) & jnp.logical_not(away) & (cs == c)
        p_src.append((device_at(xs, ys, zs, cs), same))
    member = zh == half
    h_dest = []
    for yd in range(2):
        for xd in range(4):
            yy, cd = 2 * yd + c, x // 2
            same = (xd == x) & (yy == y) & (cd == c)
            h_dest.append((device_at(xd, yy, z, cd), same, member & jnp.logical_not(same)))
    h_src = []
    for sq in range(2):
        for hl in range(2):
            xs, ys, cs = 2 * c + hl, 2 * sq + zh, y % 2
            same = (xs == x) & (ys == y) & (cs == c)
            h_src.append((device_at(xs, ys, z, cs), same))

    cps_p = [copy_in(prompt_k, in_pk, sem_in.at[0]), copy_in(prompt_v, in_pv, sem_in.at[1])]
    bar = pltpu.get_barrier_semaphore()

    def greet(where):
        pl.semaphore_signal(bar, inc=1, device_id=where, device_id_type=MESH)

    def greet_column(d, carry):
        greet(column((j + d) % 16))
        return carry

    for where, same in p_src + h_src:

        @pl.when(jnp.logical_not(same))
        def _():
            greet(where)

    lax.fori_loop(1, 16, greet_column, 0)
    for where in (up, down, sib):
        greet(where)
    cps_h = [
        copy_in(a, b, sem_in.at[5 + i])
        for i, (a, b) in enumerate(
            [(owners_h, owners), (hand_q_h, hand_q), (hand_k_h, hand_k), (hand_v_h, hand_v)]
        )
    ]
    cps_s = [
        copy_in(span_k, in_k, sem_in.at[2]),
        copy_in(span_v, in_v, sem_in.at[3]),
        copy_in(span_q, in_q, sem_in.at[4]),
    ]
    cps_d = [
        copy_in(a, b, sem_in.at[9 + i])
        for i, (a, b) in enumerate(
            [(plen_h, plen), (rlen_h, rlen), (dec_q_h, dec_q), (dec_k_h, dec_k), (dec_v_h, dec_v)]
        )
    ]
    cps_k = [copy_in(res_k.at[r], in_rk.at[r], sem_rk.at[r]) for r in range(4)]
    cps_v = [copy_in(res_v.at[r], in_rv.at[r], sem_rv.at[r]) for r in range(4)]

    expect = 18
    for _, same in p_dest:
        expect = expect + jnp.where(same, 0, 1)
    for _, _, go in h_dest:
        expect = expect + jnp.where(go, 1, 0)

    for cp in cps_h:
        cp.wait()
    hq = hand_q[...].astype(F32)
    hkv = jnp.concatenate([hand_k[...].astype(F32), hand_v[...].astype(F32)], axis=0)
    for cp in cps_p:
        cp.wait()
    for sq in range(2):
        wide[2 * sq] = in_pk[sq].astype(F32)
        wide[2 * sq + 1] = in_pv[sq].astype(F32)
    for sq in range(2):
        mine = jnp.where(owners[sq] == s, 1.0, 0.0)
        for hl in range(2):
            k = 2 * sq + hl
            stp[k, 0:64, :] = wide[2 * sq, pl.ds(hl, 64, stride=2), :].astype(BF16)
            stp[k, 64:128, :] = wide[2 * sq + 1, pl.ds(hl, 64, stride=2), :].astype(BF16)
            block = jnp.concatenate([hq[:, 8 * hl : 8 * hl + 8, :].reshape(32, 128), hkv], axis=0)
            stp[k, 128:176, :] = (block * mine).astype(BF16)

    pl.semaphore_wait(bar, expect)

    for k, (where, same) in enumerate(p_dest):

        @pl.when(jnp.logical_not(same))
        def _():
            pltpu.make_async_remote_copy(
                stp.at[k], rcp.at[y], p_send.at[k], p_recv, device_id=where, device_id_type=MESH
            ).start()

        @pl.when(same)
        def _():
            pltpu.make_async_copy(stp.at[k], rcp.at[y], p_recv).start()

    for cp in cps_s:
        cp.wait()
    for sq in range(2):
        wide[sq, 0:64, :] = in_k[sq].astype(F32).reshape(64, 128)
        wide[sq, 64:128, :] = in_v[sq].astype(F32).reshape(64, 128)
    for sq in range(2):
        for h in range(8):
            stn[8 * sq + h] = jnp.concatenate(
                [wide[sq, pl.ds(h, 8, stride=8), :], wide[sq, pl.ds(64 + h, 8, stride=8), :]], axis=0
            ).astype(BF16)

    def send_n(d, carry):
        jj = (j + d) % 16
        pltpu.make_async_remote_copy(
            stn.at[jj], rcn.at[j], n_send, n_recv, device_id=column(jj), device_id_type=MESH
        ).start()
        return carry

    lax.fori_loop(1, 16, send_n, 0)
    pltpu.make_async_copy(stn.at[j], rcn.at[j], n_recv).start()

    for sq in range(2):
        for hh in range(4):
            two = in_q[sq, :, 16 * hh : 16 * hh + 16, :].astype(F32)
            for e in range(2):
                h = 2 * hh + e
                stq[8 * sq + h] = two[:, 8 * e : 8 * e + 8, :].reshape(64, 128).astype(BF16)

    def send_q(d, carry):
        jj = (j + d) % 16
        pltpu.make_async_remote_copy(
            stq.at[jj], rcq.at[j], q_send, q_recv, device_id=column(jj), device_id_type=MESH
        ).start()
        return carry

    lax.fori_loop(1, 16, send_q, 0)
    pltpu.make_async_copy(stq.at[j], rcq.at[j], q_recv).start()

    row = lax.broadcasted_iota(jnp.int32, (1024, 128), 0)
    lane = lax.broadcasted_iota(jnp.int32, (1024, 128), 1)
    dmat[...] = (
        32 * (row // 64) + (row % 64) // 8 - 32 * (lane // 8) - lane % 8
    ).astype(F32)
    top[...] = jnp.full((1024, 128), LOW, F32)
    total[...] = jnp.zeros((1024, 128), F32)
    mixed[...] = jnp.zeros((1024, 128), F32)

    for cp in cps_d:
        cp.wait()
    dkpad[...] = jnp.zeros((128, 128), BF16)
    dvpad[...] = jnp.zeros((128, 128), BF16)
    dkpad[0:32, :] = dec_k[...]
    dvpad[0:32, :] = dec_v[...]
    col = lax.broadcasted_iota(jnp.int32, (8, 2048), 1)
    row64 = lax.broadcasted_iota(jnp.int32, (64, 128), 0)
    lane64 = lax.broadcasted_iota(jnp.int32, (64, 128), 1)
    own_ok = (lane64 % 2 == (row64 // 8) % 2) & ((lane64 % 8) // 2 <= row64 // 16)
    for r in range(4):
        cps_k[r].wait()
        qr = dec_q[r]
        sc = dot_t(qr, in_rk[r])
        inside = col // 2 < rlen[r]
        b0 = jnp.where(inside & (col % 2 == 0), 0.0, LOW)
        b1 = jnp.where(inside & (col % 2 == 1), 0.0, LOW)
        both = jnp.concatenate([b0, b1], axis=0)
        sc = sc + jnp.concatenate([both] * 4, axis=0)
        so = jnp.where(own_ok & (lane64 // 8 == r), dot_t(qr, dkpad[...]), LOW)
        mx = jnp.maximum(jnp.max(sc, axis=1, keepdims=True), jnp.max(so, axis=1, keepdims=True))
        ps = jnp.exp2((sc - mx) * SCALE)
        po = jnp.exp2((so - mx) * SCALE)
        den = jnp.sum(ps, axis=1, keepdims=True) + jnp.sum(po, axis=1, keepdims=True)
        cps_v[r].wait()
        num = dot(ps.astype(BF16), in_rv[r]) + dot(po.astype(BF16), dvpad[...])
        resbuf[r] = (num / den).astype(BF16)
    cp_res = pltpu.make_async_copy(resbuf, out_r, sem_out.at[0])
    cp_res.start()

    def recv(ref, sem):
        pltpu.make_async_remote_copy(ref, ref, h_send.at[0], sem, device_id=sib, device_id_type=MESH).wait_recv()

    parts = (pl.ds(0, 256), pl.ds(256, 288), pl.ds(544, 272))
    last = (pl.ds(0, 256), pl.ds(256, 144), pl.ds(400, 144), pl.ds(544, 272))

    def send_on(src, dst, part, where, lane_index, sem):
        pltpu.make_async_remote_copy(
            kv.at[src, c, part], kv.at[dst, c, part],
            ring_send.at[lane_index], ring_recv.at[dst, sem], device_id=where, device_id_type=MESH,
        ).start()

    def share(slot, part):
        pltpu.make_async_remote_copy(
            kv.at[slot, c, part], kv.at[slot, c, part],
            sib_send, sib_recv.at[slot], device_id=sib, device_id_type=MESH,
        ).start()

    def arrive(slot, part, sem):
        recv(kv.at[slot, c, part], ring_recv.at[slot, sem])

    def shared(slot):
        recv(kv.at[slot, 1 - c], sib_recv.at[slot])

    recv(rcn, n_recv)
    new = rcn[...].astype(F32)
    kv[0, c, 0:128, :] = new[:, 0:8, :].reshape(128, 128).astype(BF16)
    kv[0, c, 128:256, :] = new[:, 8:16, :].reshape(128, 128).astype(BF16)
    send_on(0, 1, parts[0], up, 0, 0)
    send_on(0, 2, parts[0], down, 1, 0)
    recv(rcp, p_recv)
    handed = rcp[0, 128:176, :].astype(F32)
    for ys in range(4):
        kv[0, c, 256 + 64 * ys : 320 + 64 * ys, :] = rcp[ys, 0:64, :]
        kv[0, c, 512 + 64 * ys : 576 + 64 * ys, :] = rcp[ys, 64:128, :]
        if ys:
            handed = handed + rcp[ys, 128:176, :].astype(F32)
    kv[0, c, 768:816, :] = handed.astype(BF16)
    for part in (1, 2):
        send_on(0, 1, parts[part], up, 0, part)
        send_on(0, 2, parts[part], down, 1, part)
    share(0, pl.ds(0, 816))

    plen_here = plen[seq]
    lane1 = lax.broadcasted_iota(jnp.int32, (1, 128), 1)
    lane_pos = 1024 * (lane1 // 64) + lane1 % 64
    z_of = [z, (z + 7) % 8, (z + 1) % 8, (z + 6) % 8, (z + 2) % 8, (z + 5) % 8, (z + 3) % 8, (z + 4) % 8]

    def prompt_bias(slot, cc):
        zz = z_of[slot]
        near = 256 * (cc + 2 * seq) + 64 * (zz % 4)
        far = 256 * (cc + 2 * (1 - seq)) + 64 * (3 - zz % 4)
        off = jnp.where(zz // 4 == half, near, far)
        return [jnp.where(lane_pos + (off + 2048 * e) < plen_here, 0.0, LOW) for e in range(2)]

    def process(blocks, after=None):
        rows = ROWS if after is not None else 1024
        bias = [prompt_bias(slot, cc) for slot, cc in blocks]
        limit = [
            (512 * (2 * (z_of[slot] // 4) + cc - t) + 8 * (z_of[slot] % 4 - zl)).astype(F32)
            for slot, cc in blocks
        ]

        def tile(n):
            rs = pl.ds(n * rows, rows)
            q = rcq[n * (rows // 64) : (n + 1) * (rows // 64), :, :].reshape(rows, 128)
            keys = jnp.concatenate(
                [kv[slot, cc, part, :] for slot, cc in blocks for part in (slice(256, 512), slice(0, 128))], axis=0
            )
            values = jnp.concatenate(
                [kv[slot, cc, part, :] for slot, cc in blocks for part in (slice(512, 768), slice(128, 256))], axis=0
            )
            sc = dot_t(q, keys)
            ss = []
            for i in range(len(blocks)):
                ss.append(sc[:, 384 * i : 384 * i + 128] + bias[i][0])
                ss.append(sc[:, 384 * i + 128 : 384 * i + 256] + bias[i][1])
                ss.append(jnp.where(dmat[rs, :] >= limit[i], sc[:, 384 * i + 256 : 384 * i + 384], LOW))
            mx = ss[0]
            for v in ss[1:]:
                mx = jnp.maximum(mx, v)
            old = top[rs, :]
            now = jnp.maximum(old, jnp.max(mx, axis=1, keepdims=True))
            shrink = jnp.exp2((old - now) * SCALE)
            top[rs, :] = now
            ps = [jnp.exp2((v - now) * SCALE) for v in ss]
            su = ps[0]
            for v in ps[1:]:
                su = su + v
            p = jnp.concatenate([v.astype(BF16) for v in ps], axis=1)
            mixed[rs, :] = mixed[rs, :] * shrink + dot(p, values)
            total[rs, :] = total[rs, :] * shrink + su

        for n in range(1024 // rows):
            tile(n)
            if after is not None:
                after(n)

    def send_o(n):
        rs = pl.ds(n * ROWS, ROWS)
        count = ROWS // 64
        part = mixed[rs, :] / jnp.sum(total[rs, :], axis=1, keepdims=True)
        sto[n * count : (n + 1) * count] = part.astype(BF16).reshape(count, 64, 128)

        def one(d, carry):
            jj = n * count + (j + d) % count

            @pl.when(jj != j)
            def _():
                pltpu.make_async_remote_copy(
                    sto.at[jj], rco.at[j], o_send, o_recv, device_id=column(jj), device_id_type=MESH
                ).start()

            @pl.when(jj == j)
            def _():
                pltpu.make_async_copy(sto.at[jj], rco.at[j], o_recv).start()

            return carry

        lax.fori_loop(0, count, one, 0)

    def theirs(slots):
        for slot in slots:
            shared(slot)
        process([(slot, 1 - c) for slot in slots])

    recv(rcq, q_recv)
    process([(0, c)])
    for a in (1, 2, 3):
        plus, minus = 2 * a - 1, 2 * a
        for part in (0, 1, 2):
            arrive(plus, parts[part], part)
            if a < 3:
                send_on(plus, plus + 2, parts[part], up, 0, part)
            elif part < 2:
                send_on(plus, 7, last[part], up, 2, part)
            arrive(minus, parts[part], part)
            if a < 3:
                send_on(minus, minus + 2, parts[part], down, 1, part)
            elif part > 0:
                send_on(minus, 7, last[part + 1], down, 3, part + 1)
            if part == 2:
                share(plus, pl.ds(0, 816))
                share(minus, pl.ds(0, 816))
            if part < 2 and a > 1:
                theirs([2 * a - 3 + part])
            elif part == 0:
                theirs([0])
        process([(plus, c), (minus, c)])
    arrive(7, last[0], 0)
    arrive(7, last[1], 1)
    share(7, pl.ds(0, 400))
    theirs([5, 6])
    arrive(7, last[2], 2)
    arrive(7, last[3], 3)
    share(7, pl.ds(400, 416))
    process([(7, c)])
    shared(7)
    process([(7, 1 - c)], send_o)

    hsum = jnp.zeros((48, 128), F32)
    for slot in range(8):
        for cc in range(2):
            hsum = hsum + kv[slot, cc, 768:816, :].astype(F32)
    qh = hsum[0:32, :].astype(BF16)
    dkpad[...] = jnp.zeros((128, 128), BF16)
    dvpad[...] = jnp.zeros((128, 128), BF16)
    zero8 = jnp.zeros((8, 128), F32)
    dkpad[0:16, :] = jnp.concatenate([hsum[32:40, :], zero8], axis=0).astype(BF16)
    dvpad[0:16, :] = jnp.concatenate([hsum[40:48, :], zero8], axis=0).astype(BF16)
    row32 = lax.broadcasted_iota(jnp.int32, (32, 128), 0)
    lane32 = lax.broadcasted_iota(jnp.int32, (32, 128), 1)
    ok = (lane32 < 8) & (lane32 % 2 == x % 2) & (lane32 // 2 <= row32 // 8)
    so = jnp.where(ok, dot_t(qh, dkpad[...]), LOW)
    ss = []
    for slot in range(8):
        for cc in range(2):
            sc = dot_t(qh, jnp.concatenate([kv[slot, cc, 256:512, :], kv[slot, cc, 0:128, :]], axis=0))
            bias = prompt_bias(slot, cc)
            ss.append([sc[:, 0:128] + bias[0], sc[:, 128:256] + bias[1], sc[:, 256:384]])
    mx = so
    for three in ss:
        for v in three:
            mx = jnp.maximum(mx, v)
    mx = jnp.max(mx, axis=1, keepdims=True)
    po = jnp.exp2((so - mx) * SCALE)
    su = po
    num = dot(po.astype(BF16), dvpad[...])
    for i, three in enumerate(ss):
        ps = [jnp.exp2((v - mx) * SCALE) for v in three]
        su = su + ps[0] + ps[1] + ps[2]
        p = jnp.concatenate([v.astype(BF16) for v in ps], axis=1)
        num = num + dot(
            p, jnp.concatenate([kv[i // 2, i % 2, 512:768, :], kv[i // 2, i % 2, 128:256, :]], axis=0)
        )
    sth[...] = (num / jnp.sum(su, axis=1, keepdims=True)).astype(BF16)
    slot_h = seq * 2 + x % 2
    for k, (where, same, go) in enumerate(h_dest):

        @pl.when(go)
        def _():
            pltpu.make_async_remote_copy(
                sth, rch.at[slot_h], h_send.at[k], h_recv, device_id=where, device_id_type=MESH
            ).start()

        @pl.when(member & same)
        def _():
            pltpu.make_async_copy(sth, rch.at[slot_h], h_recv).start()

    def sent(ref, sem):
        pltpu.make_async_remote_copy(ref, ref, sem, h_recv, device_id=sib, device_id_type=MESH).wait_send()

    for k, (_, same) in enumerate(p_dest):

        @pl.when(jnp.logical_not(same))
        def _():
            sent(stp.at[k], p_send.at[k])

    sent(stn.at[pl.ds(0, 15)], n_send)
    sent(stq.at[pl.ds(0, 15)], q_send)
    sent(kv.at[pl.ds(0, 3), 0], ring_send.at[0])
    sent(kv.at[pl.ds(0, 3), 0], ring_send.at[1])
    sent(kv.at[0, 0, pl.ds(0, 400)], ring_send.at[2])
    sent(kv.at[0, 0, pl.ds(400, 416)], ring_send.at[3])
    sent(kv.at[pl.ds(0, 8), 0], sib_send)

    recv(rch, h_recv)
    heads = []
    for hl in range(2):
        acc = jnp.zeros((32, 128), F32)
        for sq in range(2):
            mine = jnp.where(owners[sq] == s, 1.0, 0.0)
            acc = acc + rch[2 * sq + hl].astype(F32) * mine
        heads.append(acc.reshape(4, 8, 128))
    hbuf[...] = jnp.concatenate(heads, axis=1).astype(BF16)
    cp_hand = pltpu.make_async_copy(hbuf, out_h, sem_out.at[1])
    cp_hand.start()

    recv(rco, o_recv)

    for k, (_, same, go) in enumerate(h_dest):

        @pl.when(go)
        def _():
            sent(sth, h_send.at[k])

    sent(sto.at[pl.ds(0, 15)], o_send)
    cp_res.wait()
    cp_hand.wait()


def place(got, res, hand, out_p, out_r, out_h, pieces, whole, vres, vhand, sem_in, sem_out):
    in_r = pltpu.make_async_copy(res, vres, sem_in.at[2])
    in_h = pltpu.make_async_copy(hand, vhand, sem_in.at[3])
    cp_r = pltpu.make_async_copy(vres, out_r, sem_out.at[2])
    cp_h = pltpu.make_async_copy(vhand, out_h, sem_out.at[3])
    loads = [
        pltpu.make_async_copy(got.at[pl.ds(8 * sq, 8)], pieces.at[pl.ds(8 * sq, 8)], sem_in.at[sq])
        for sq in range(2)
    ]
    for cp in loads:
        cp.start()
    in_r.start()
    in_h.start()
    stores = []
    for sq in range(2):
        loads[sq].wait()
        for hh in range(4):
            a = pieces[8 * sq + 2 * hh].astype(F32).reshape(8, 8, 128)
            b = pieces[8 * sq + 2 * hh + 1].astype(F32).reshape(8, 8, 128)
            whole[sq, :, 16 * hh : 16 * hh + 16, :] = jnp.concatenate([a, b], axis=1).astype(BF16)
        cp = pltpu.make_async_copy(whole.at[sq], out_p.at[sq], sem_out.at[sq])
        cp.start()
        stores.append(cp)
    in_r.wait()
    cp_r.start()
    in_h.wait()
    cp_h.start()
    for cp in stores:
        cp.wait()
    cp_r.wait()
    cp_h.wait()


def on_device(
    prompt_lengths, owners, span_q, span_k, span_v, prompt_keys, prompt_values, res_lengths,
    res_keys, res_values, dec_q, dec_k, dec_v, hand_q, hand_k, hand_v,
):
    hbm = pl.BlockSpec(memory_space=pltpu.HBM)
    dma = pltpu.SemaphoreType.DMA
    out = pl.pallas_call(
        kernel,
        out_shape=(
            jax.ShapeDtypeStruct((16, 64, 128), BF16),
            jax.ShapeDtypeStruct((4, 64, 128), BF16),
            jax.ShapeDtypeStruct((4, 16, 128), BF16),
        ),
        in_specs=[hbm] * 16,
        out_specs=(hbm, hbm, hbm),
        scratch_shapes=[
            pltpu.VMEM((2, 8, 64, 128), BF16),
            pltpu.VMEM((2, 8, 8, 128), BF16),
            pltpu.VMEM((2, 8, 8, 128), BF16),
            pltpu.VMEM((2, 128, 128), BF16),
            pltpu.VMEM((2, 128, 128), BF16),
            pltpu.VMEM((4, 2048, 128), BF16),
            pltpu.VMEM((4, 2048, 128), BF16),
            pltpu.SMEM((2,), jnp.int32),
            pltpu.SMEM((2,), jnp.int32),
            pltpu.SMEM((4,), jnp.int32),
            pltpu.VMEM((4, 64, 128), BF16),
            pltpu.VMEM((32, 128), BF16),
            pltpu.VMEM((32, 128), BF16),
            pltpu.VMEM((4, 16, 128), BF16),
            pltpu.VMEM((8, 128), BF16),
            pltpu.VMEM((8, 128), BF16),
            pltpu.VMEM((4, 16, 128), BF16),
            pltpu.VMEM((4, 128, 128), F32),
            pltpu.VMEM((16, 16, 128), BF16),
            pltpu.VMEM((16, 16, 128), BF16),
            pltpu.VMEM((16, 64, 128), BF16),
            pltpu.VMEM((16, 64, 128), BF16),
            pltpu.VMEM((4, 176, 128), BF16),
            pltpu.VMEM((4, 176, 128), BF16),
            pltpu.VMEM((8, 2, 816, 128), BF16),
            pltpu.VMEM((1024, 128), F32),
            pltpu.VMEM((1024, 128), F32),
            pltpu.VMEM((1024, 128), F32),
            pltpu.VMEM((1024, 128), F32),
            pltpu.VMEM((16, 64, 128), BF16),
            pltpu.VMEM((32, 128), BF16),
            pltpu.VMEM((4, 32, 128), BF16),
            pltpu.VMEM((4, 64, 128), BF16),
            pltpu.VMEM((128, 128), BF16),
            pltpu.VMEM((128, 128), BF16),
            dma((14,)), dma((4,)), dma((4,)), dma((2,)),
            dma, dma, dma, dma, dma((4,)), dma, dma((4,)), dma((8, 4)), dma, dma((8,)),
            dma, dma, dma((8,)), dma,
        ],
        compiler_params=pltpu.CompilerParams(
            collective_id=0, has_side_effects=True, vmem_limit_bytes=64 << 20
        ),
        name="spanned",
    )(
        prompt_lengths, owners, res_lengths, span_q, span_k, span_v,
        prompt_keys.reshape(2, 128, 128), prompt_values.reshape(2, 128, 128),
        res_keys.reshape(4, 2048, 128), res_values.reshape(4, 2048, 128),
        dec_q.reshape(4, 64, 128), dec_k.reshape(32, 128), dec_v.reshape(32, 128),
        hand_q.reshape(4, 16, 128), hand_k.reshape(8, 128), hand_v.reshape(8, 128),
    )
    any_space = pl.BlockSpec(memory_space=pl.ANY)
    prefill_out, res_out, hand_out = pl.pallas_call(
        place,
        out_shape=(
            jax.ShapeDtypeStruct((2, 8, 64, 128), BF16),
            jax.ShapeDtypeStruct((4, 64, 128), BF16),
            jax.ShapeDtypeStruct((4, 16, 128), BF16),
        ),
        in_specs=[any_space] * 3,
        out_specs=(any_space,) * 3,
        scratch_shapes=[
            pltpu.VMEM((16, 64, 128), BF16), pltpu.VMEM((2, 8, 64, 128), BF16), pltpu.VMEM((4, 64, 128), BF16),
            pltpu.VMEM((4, 16, 128), BF16), dma((4,)), dma((4,)),
        ],
        compiler_params=pltpu.CompilerParams(vmem_limit_bytes=64 << 20),
        name="place",
    )(*out)
    return (prefill_out, res_out.reshape(4, 4, 16, 128), hand_out.reshape(1, 4, 16, 128))


def solution(mesh):
    cache = P("section", None, "tensor", None)
    span = P(None, ("tensor", "section"), None, None)
    prompt = P(None, "section", "tensor", None)
    return jax.shard_map(
        on_device,
        mesh=mesh,
        in_specs=(P(), P(), span, span, span, prompt, prompt, P("section")) + (cache,) * 8,
        out_specs=(span, cache, cache),
        check_vma=False,
    )
```

```python
import jax
import jax.numpy as jnp
from jax import lax
from jax.experimental import pallas as pl
from jax.experimental.pallas import tpu as pltpu
from jax.sharding import PartitionSpec as P

MESH = pl.DeviceIdType.MESH
F32 = jnp.float32
BF16 = jnp.bfloat16
SCALE = 128 ** -0.5 * 1.4426950408889634
LOW = -1e30
ROWS = 512


def device_at(x, y, z, c):
    return ((z // 4) * 2 + c, y * 16 + x * 4 + z % 4)


def dot_t(a, b):
    return lax.dot_general(a, b, (((1,), (1,)), ((), ())), preferred_element_type=F32)


def dot(a, b):
    return jnp.dot(a, b, preferred_element_type=F32)


def kernel(
    plen_h, owners_h, rlen_h, span_q, span_k, span_v, prompt_k, prompt_v, res_k, res_v,
    dec_q_h, dec_k_h, dec_v_h, hand_q_h, hand_k_h, hand_v_h,
    rco, out_r, out_h,
    in_q, in_k, in_v, in_pk, in_pv, in_rk, in_rv,
    plen, owners, rlen, dec_q, dec_k, dec_v, hand_q, hand_k, hand_v, hbuf,
    wide, stn, rcn, stq, rcq, stp, rcp, kv, top, total, mixed, dmat, sto, sth, rch,
    resbuf, dkpad, dvpad,
    sem_in, sem_rk, sem_rv, sem_out,
    n_send, n_recv, q_send, q_recv, p_send, p_recv, ring_send, ring_recv, sib_send, sib_recv,
    o_send, o_recv, h_send, h_recv,
):
    t = lax.axis_index("tensor")
    s = lax.axis_index("section")
    zh, c = t // 2, t % 2
    x, y, zl = (s // 4) % 4, s // 16, s % 4
    z = zh * 4 + zl
    j = s // 4
    seq, half = y // 2, y % 2

    def copy_in(a, b, sem):
        cp = pltpu.make_async_copy(a, b, sem)
        cp.start()
        return cp

    def column(jj):
        return device_at(jj % 4, jj // 4, z, c)

    up = device_at(x, y, (z + 1) % 8, c)
    down = device_at(x, y, (z + 7) % 8, c)
    sib = device_at(x, y, z, 1 - c)

    p_dest = []
    for sq in range(2):
        for hl in range(2):
            xd, yd, cd = 2 * c + hl, 2 * sq + zh, x % 2
            cross = x // 2 != sq
            zd = jnp.where(cross, 7 - z, z)
            same = (xd == x) & (yd == y) & jnp.logical_not(cross) & (cd == c)
            p_dest.append((device_at(xd, yd, zd, cd), same))
    p_src = []
    away = zh != half
    for ys in range(4):
        xs, cs = 2 * jnp.where(away, 1 - seq, seq) + c, x // 2
        zs = jnp.where(away, 7 - z, z)
        same = (xs == x) & (ys == y) & jnp.logical_not(away) & (cs == c)
        p_src.append((device_at(xs, ys, zs, cs), same))
    member = zh == half
    h_dest = []
    for yd in range(2):
        for xd in range(4):
            yy, cd = 2 * yd + c, x // 2
            same = (xd == x) & (yy == y) & (cd == c)
            h_dest.append((device_at(xd, yy, z, cd), same, member & jnp.logical_not(same)))
    h_src = []
    for sq in range(2):
        for hl in range(2):
            xs, ys, cs = 2 * c + hl, 2 * sq + zh, y % 2
            same = (xs == x) & (ys == y) & (cs == c)
            h_src.append((device_at(xs, ys, z, cs), same))

    cps_p = [copy_in(prompt_k, in_pk, sem_in.at[0]), copy_in(prompt_v, in_pv, sem_in.at[1])]
    cps_h = [
        copy_in(a, b, sem_in.at[5 + i])
        for i, (a, b) in enumerate(
            [(owners_h, owners), (hand_q_h, hand_q), (hand_k_h, hand_k), (hand_v_h, hand_v)]
        )
    ]
    bar = pltpu.get_barrier_semaphore()

    def greet(where):
        pl.semaphore_signal(bar, inc=1, device_id=where, device_id_type=MESH)

    def greet_column(d, carry):
        greet(column((j + d) % 16))
        return carry

    for where, same in p_src + h_src:

        @pl.when(jnp.logical_not(same))
        def _():
            greet(where)

    lax.fori_loop(1, 16, greet_column, 0)
    for where in (up, down, sib):
        greet(where)
    cps_s = [
        copy_in(span_k, in_k, sem_in.at[2]),
        copy_in(span_v, in_v, sem_in.at[3]),
        copy_in(span_q, in_q, sem_in.at[4]),
    ]
    cps_d = [
        copy_in(a, b, sem_in.at[9 + i])
        for i, (a, b) in enumerate(
            [(plen_h, plen), (rlen_h, rlen), (dec_q_h, dec_q), (dec_k_h, dec_k), (dec_v_h, dec_v)]
        )
    ]
    cps_k = [copy_in(res_k.at[r], in_rk.at[r], sem_rk.at[r]) for r in range(4)]
    cps_v = [copy_in(res_v.at[r], in_rv.at[r], sem_rv.at[r]) for r in range(4)]

    expect = 18
    for _, same in p_dest:
        expect = expect + jnp.where(same, 0, 1)
    for _, _, go in h_dest:
        expect = expect + jnp.where(go, 1, 0)

    for cp in cps_h:
        cp.wait()
    hq = hand_q[...].astype(F32)
    hkv = jnp.concatenate([hand_k[...].astype(F32), hand_v[...].astype(F32)], axis=0)
    for cp in cps_p:
        cp.wait()
    for sq in range(2):
        wide[2 * sq] = in_pk[sq].astype(F32)
        wide[2 * sq + 1] = in_pv[sq].astype(F32)
    for sq in range(2):
        mine = jnp.where(owners[sq] == s, 1.0, 0.0)
        for hl in range(2):
            k = 2 * sq + hl
            stp[k, 0:64, :] = wide[2 * sq, pl.ds(hl, 64, stride=2), :].astype(BF16)
            stp[k, 64:128, :] = wide[2 * sq + 1, pl.ds(hl, 64, stride=2), :].astype(BF16)
            block = jnp.concatenate([hq[:, 8 * hl : 8 * hl + 8, :].reshape(32, 128), hkv], axis=0)
            stp[k, 128:176, :] = (block * mine).astype(BF16)

    pl.semaphore_wait(bar, expect)

    for k, (where, same) in enumerate(p_dest):

        @pl.when(jnp.logical_not(same))
        def _():
            pltpu.make_async_remote_copy(
                stp.at[k], rcp.at[y], p_send.at[k], p_recv, device_id=where, device_id_type=MESH
            ).start()

        @pl.when(same)
        def _():
            pltpu.make_async_copy(stp.at[k], rcp.at[y], p_recv).start()

    for cp in cps_s:
        cp.wait()
    for sq in range(2):
        wide[sq, 0:64, :] = in_k[sq].astype(F32).reshape(64, 128)
        wide[sq, 64:128, :] = in_v[sq].astype(F32).reshape(64, 128)
    for sq in range(2):
        for h in range(8):
            stn[8 * sq + h] = jnp.concatenate(
                [wide[sq, pl.ds(h, 8, stride=8), :], wide[sq, pl.ds(64 + h, 8, stride=8), :]], axis=0
            ).astype(BF16)

    def send_n(d, carry):
        jj = (j + d) % 16
        pltpu.make_async_remote_copy(
            stn.at[jj], rcn.at[j], n_send, n_recv, device_id=column(jj), device_id_type=MESH
        ).start()
        return carry

    lax.fori_loop(1, 16, send_n, 0)
    pltpu.make_async_copy(stn.at[j], rcn.at[j], n_recv).start()

    for sq in range(2):
        for hh in range(4):
            two = in_q[sq, :, 16 * hh : 16 * hh + 16, :].astype(F32)
            for e in range(2):
                h = 2 * hh + e
                stq[8 * sq + h] = two[:, 8 * e : 8 * e + 8, :].reshape(64, 128).astype(BF16)

    def send_q(d, carry):
        jj = (j + d) % 16
        pltpu.make_async_remote_copy(
            stq.at[jj], rcq.at[j], q_send, q_recv, device_id=column(jj), device_id_type=MESH
        ).start()
        return carry

    lax.fori_loop(1, 16, send_q, 0)
    pltpu.make_async_copy(stq.at[j], rcq.at[j], q_recv).start()

    row = lax.broadcasted_iota(jnp.int32, (1024, 128), 0)
    lane = lax.broadcasted_iota(jnp.int32, (1024, 128), 1)
    dmat[...] = (
        32 * (row // 64) + (row % 64) // 8 - 32 * (lane // 8) - lane % 8
    ).astype(F32)
    top[...] = jnp.full((1024, 128), LOW, F32)
    total[...] = jnp.zeros((1024, 128), F32)
    mixed[...] = jnp.zeros((1024, 128), F32)

    for cp in cps_d:
        cp.wait()
    dkpad[...] = jnp.zeros((128, 128), BF16)
    dvpad[...] = jnp.zeros((128, 128), BF16)
    dkpad[0:32, :] = dec_k[...]
    dvpad[0:32, :] = dec_v[...]
    col = lax.broadcasted_iota(jnp.int32, (8, 2048), 1)
    row64 = lax.broadcasted_iota(jnp.int32, (64, 128), 0)
    lane64 = lax.broadcasted_iota(jnp.int32, (64, 128), 1)
    own_ok = (lane64 % 2 == (row64 // 8) % 2) & ((lane64 % 8) // 2 <= row64 // 16)
    for r in range(4):
        cps_k[r].wait()
        qr = dec_q[r]
        sc = dot_t(qr, in_rk[r])
        inside = col // 2 < rlen[r]
        b0 = jnp.where(inside & (col % 2 == 0), 0.0, LOW)
        b1 = jnp.where(inside & (col % 2 == 1), 0.0, LOW)
        both = jnp.concatenate([b0, b1], axis=0)
        sc = sc + jnp.concatenate([both] * 4, axis=0)
        so = jnp.where(own_ok & (lane64 // 8 == r), dot_t(qr, dkpad[...]), LOW)
        mx = jnp.maximum(jnp.max(sc, axis=1, keepdims=True), jnp.max(so, axis=1, keepdims=True))
        ps = jnp.exp2((sc - mx) * SCALE)
        po = jnp.exp2((so - mx) * SCALE)
        den = jnp.sum(ps, axis=1, keepdims=True) + jnp.sum(po, axis=1, keepdims=True)
        cps_v[r].wait()
        num = dot(ps.astype(BF16), in_rv[r]) + dot(po.astype(BF16), dvpad[...])
        resbuf[r] = (num / den).astype(BF16)
    cp_res = pltpu.make_async_copy(resbuf, out_r, sem_out.at[0])
    cp_res.start()

    def recv(ref, sem):
        pltpu.make_async_remote_copy(ref, ref, h_send.at[0], sem, device_id=sib, device_id_type=MESH).wait_recv()

    parts = (pl.ds(0, 256), pl.ds(256, 288), pl.ds(544, 272))
    last = (pl.ds(0, 256), pl.ds(256, 144), pl.ds(400, 144), pl.ds(544, 272))

    def send_on(src, dst, part, where, lane_index, sem):
        pltpu.make_async_remote_copy(
            kv.at[src, c, part], kv.at[dst, c, part],
            ring_send.at[lane_index], ring_recv.at[dst, sem], device_id=where, device_id_type=MESH,
        ).start()

    def share(slot, part):
        pltpu.make_async_remote_copy(
            kv.at[slot, c, part], kv.at[slot, c, part],
            sib_send, sib_recv.at[slot], device_id=sib, device_id_type=MESH,
        ).start()

    def arrive(slot, part, sem):
        recv(kv.at[slot, c, part], ring_recv.at[slot, sem])

    def shared(slot):
        recv(kv.at[slot, 1 - c], sib_recv.at[slot])

    recv(rcn, n_recv)
    new = rcn[...].astype(F32)
    kv[0, c, 0:128, :] = new[:, 0:8, :].reshape(128, 128).astype(BF16)
    kv[0, c, 128:256, :] = new[:, 8:16, :].reshape(128, 128).astype(BF16)
    send_on(0, 1, parts[0], up, 0, 0)
    send_on(0, 2, parts[0], down, 1, 0)
    recv(rcp, p_recv)
    handed = rcp[0, 128:176, :].astype(F32)
    for ys in range(4):
        kv[0, c, 256 + 64 * ys : 320 + 64 * ys, :] = rcp[ys, 0:64, :]
        kv[0, c, 512 + 64 * ys : 576 + 64 * ys, :] = rcp[ys, 64:128, :]
        if ys:
            handed = handed + rcp[ys, 128:176, :].astype(F32)
    kv[0, c, 768:816, :] = handed.astype(BF16)
    for part in (1, 2):
        send_on(0, 1, parts[part], up, 0, part)
        send_on(0, 2, parts[part], down, 1, part)
    share(0, pl.ds(0, 816))

    plen_here = plen[seq]
    lane1 = lax.broadcasted_iota(jnp.int32, (1, 128), 1)
    lane_pos = 1024 * (lane1 // 64) + lane1 % 64
    z_of = [z, (z + 7) % 8, (z + 1) % 8, (z + 6) % 8, (z + 2) % 8, (z + 5) % 8, (z + 3) % 8, (z + 4) % 8]

    def prompt_bias(slot, cc):
        zz = z_of[slot]
        near = 256 * (cc + 2 * seq) + 64 * (zz % 4)
        far = 256 * (cc + 2 * (1 - seq)) + 64 * (3 - zz % 4)
        off = jnp.where(zz // 4 == half, near, far)
        return [jnp.where(lane_pos + (off + 2048 * e) < plen_here, 0.0, LOW) for e in range(2)]

    def process(blocks, after=None):
        rows = 1024 if after is None and len(blocks) == 1 else ROWS
        bias = [prompt_bias(slot, cc) for slot, cc in blocks]
        limit = [
            (512 * (2 * (z_of[slot] // 4) + cc - t) + 8 * (z_of[slot] % 4 - zl)).astype(F32)
            for slot, cc in blocks
        ]

        keys = jnp.concatenate(
            [kv[slot, cc, part, :] for slot, cc in blocks for part in (slice(256, 512), slice(0, 128))], axis=0
        )
        values = jnp.concatenate(
            [kv[slot, cc, part, :] for slot, cc in blocks for part in (slice(512, 768), slice(128, 256))], axis=0
        )

        def scores(n):
            return dot_t(rcq[n * (rows // 64) : (n + 1) * (rows // 64), :, :].reshape(rows, 128), keys)

        def weigh(n, sc):
            rs = pl.ds(n * rows, rows)
            ss = []
            for i in range(len(blocks)):
                ss.append(sc[:, 384 * i : 384 * i + 128] + bias[i][0])
                ss.append(sc[:, 384 * i + 128 : 384 * i + 256] + bias[i][1])
                ss.append(jnp.where(dmat[rs, :] >= limit[i], sc[:, 384 * i + 256 : 384 * i + 384], LOW))
            mx = ss[0]
            for v in ss[1:]:
                mx = jnp.maximum(mx, v)
            old = top[rs, :]
            now = jnp.maximum(old, jnp.max(mx, axis=1, keepdims=True))
            shrink = jnp.exp2((old - now) * SCALE)
            top[rs, :] = now
            ps = [jnp.exp2((v - now) * SCALE) for v in ss]
            su = ps[0]
            for v in ps[1:]:
                su = su + v
            total[rs, :] = total[rs, :] * shrink + su
            return shrink, jnp.concatenate([v.astype(BF16) for v in ps], axis=1)

        sc = scores(0)
        for n in range(1024 // rows):
            nxt = scores(n + 1) if n + 1 < 1024 // rows else None
            shrink, p = weigh(n, sc)
            rs = pl.ds(n * rows, rows)
            mixed[rs, :] = mixed[rs, :] * shrink + dot(p, values)
            if after is not None:
                after(n)
            sc = nxt

    def send_o(n):
        rs = pl.ds(n * ROWS, ROWS)
        count = ROWS // 64
        part = mixed[rs, :] / jnp.sum(total[rs, :], axis=1, keepdims=True)
        sto[n * count : (n + 1) * count] = part.astype(BF16).reshape(count, 64, 128)

        def one(d, carry):
            jj = n * count + (j + d) % count

            @pl.when(jj != j)
            def _():
                pltpu.make_async_remote_copy(
                    sto.at[jj], rco.at[j], o_send, o_recv, device_id=column(jj), device_id_type=MESH
                ).start()

            @pl.when(jj == j)
            def _():
                pltpu.make_async_copy(sto.at[jj], rco.at[j], o_recv).start()

            return carry

        lax.fori_loop(0, count, one, 0)

    def theirs(slots):
        for slot in slots:
            shared(slot)
        process([(slot, 1 - c) for slot in slots])

    recv(rcq, q_recv)
    process([(0, c)])
    for a in (1, 2, 3):
        plus, minus = 2 * a - 1, 2 * a
        for part in (0, 1, 2):
            arrive(plus, parts[part], part)
            if a < 3:
                send_on(plus, plus + 2, parts[part], up, 0, part)
            elif part < 2:
                send_on(plus, 7, last[part], up, 2, part)
            arrive(minus, parts[part], part)
            if a < 3:
                send_on(minus, minus + 2, parts[part], down, 1, part)
            elif part > 0:
                send_on(minus, 7, last[part + 1], down, 3, part + 1)
            if part == 2:
                share(plus, pl.ds(0, 816))
                share(minus, pl.ds(0, 816))
            if part < 2 and a > 1:
                theirs([2 * a - 3 + part])
            elif part == 0:
                theirs([0])
        process([(plus, c), (minus, c)])
    arrive(7, last[0], 0)
    arrive(7, last[1], 1)
    share(7, pl.ds(0, 400))
    theirs([5, 6])
    arrive(7, last[2], 2)
    arrive(7, last[3], 3)
    share(7, pl.ds(400, 416))
    process([(7, c)])
    shared(7)
    process([(7, 1 - c)], send_o)

    hsum = jnp.zeros((48, 128), F32)
    for slot in range(8):
        for cc in range(2):
            hsum = hsum + kv[slot, cc, 768:816, :].astype(F32)
    qh = hsum[0:32, :].astype(BF16)
    dkpad[...] = jnp.zeros((128, 128), BF16)
    dvpad[...] = jnp.zeros((128, 128), BF16)
    zero8 = jnp.zeros((8, 128), F32)
    dkpad[0:16, :] = jnp.concatenate([hsum[32:40, :], zero8], axis=0).astype(BF16)
    dvpad[0:16, :] = jnp.concatenate([hsum[40:48, :], zero8], axis=0).astype(BF16)
    row32 = lax.broadcasted_iota(jnp.int32, (32, 128), 0)
    lane32 = lax.broadcasted_iota(jnp.int32, (32, 128), 1)
    ok = (lane32 < 8) & (lane32 % 2 == x % 2) & (lane32 // 2 <= row32 // 8)
    so = jnp.where(ok, dot_t(qh, dkpad[...]), LOW)
    ss = []
    for slot in range(8):
        for cc in range(2):
            sc = dot_t(qh, jnp.concatenate([kv[slot, cc, 256:512, :], kv[slot, cc, 0:128, :]], axis=0))
            bias = prompt_bias(slot, cc)
            ss.append([sc[:, 0:128] + bias[0], sc[:, 128:256] + bias[1], sc[:, 256:384]])
    mx = so
    for three in ss:
        for v in three:
            mx = jnp.maximum(mx, v)
    mx = jnp.max(mx, axis=1, keepdims=True)
    po = jnp.exp2((so - mx) * SCALE)
    su = po
    num = dot(po.astype(BF16), dvpad[...])
    for i, three in enumerate(ss):
        ps = [jnp.exp2((v - mx) * SCALE) for v in three]
        su = su + ps[0] + ps[1] + ps[2]
        p = jnp.concatenate([v.astype(BF16) for v in ps], axis=1)
        num = num + dot(
            p, jnp.concatenate([kv[i // 2, i % 2, 512:768, :], kv[i // 2, i % 2, 128:256, :]], axis=0)
        )
    sth[...] = (num / jnp.sum(su, axis=1, keepdims=True)).astype(BF16)
    slot_h = seq * 2 + x % 2
    for k, (where, same, go) in enumerate(h_dest):

        @pl.when(go)
        def _():
            pltpu.make_async_remote_copy(
                sth, rch.at[slot_h], h_send.at[k], h_recv, device_id=where, device_id_type=MESH
            ).start()

        @pl.when(member & same)
        def _():
            pltpu.make_async_copy(sth, rch.at[slot_h], h_recv).start()

    def sent(ref, sem):
        pltpu.make_async_remote_copy(ref, ref, sem, h_recv, device_id=sib, device_id_type=MESH).wait_send()

    for k, (_, same) in enumerate(p_dest):

        @pl.when(jnp.logical_not(same))
        def _():
            sent(stp.at[k], p_send.at[k])

    sent(stn.at[pl.ds(0, 15)], n_send)
    sent(stq.at[pl.ds(0, 15)], q_send)
    sent(kv.at[pl.ds(0, 3), 0], ring_send.at[0])
    sent(kv.at[pl.ds(0, 3), 0], ring_send.at[1])
    sent(kv.at[0, 0, pl.ds(0, 400)], ring_send.at[2])
    sent(kv.at[0, 0, pl.ds(400, 416)], ring_send.at[3])
    sent(kv.at[pl.ds(0, 8), 0], sib_send)

    recv(rch, h_recv)
    heads = []
    for hl in range(2):
        acc = jnp.zeros((32, 128), F32)
        for sq in range(2):
            mine = jnp.where(owners[sq] == s, 1.0, 0.0)
            acc = acc + rch[2 * sq + hl].astype(F32) * mine
        heads.append(acc.reshape(4, 8, 128))
    hbuf[...] = jnp.concatenate(heads, axis=1).astype(BF16)
    cp_hand = pltpu.make_async_copy(hbuf, out_h, sem_out.at[1])
    cp_hand.start()

    recv(rco, o_recv)

    for k, (_, same, go) in enumerate(h_dest):

        @pl.when(go)
        def _():
            sent(sth, h_send.at[k])

    sent(sto.at[pl.ds(0, 15)], o_send)
    cp_res.wait()
    cp_hand.wait()


def place(got, res, hand, out_p, out_r, out_h, pieces, whole, vres, vhand, sem_in, sem_out):
    in_r = pltpu.make_async_copy(res, vres, sem_in.at[2])
    in_h = pltpu.make_async_copy(hand, vhand, sem_in.at[3])
    cp_r = pltpu.make_async_copy(vres, out_r, sem_out.at[2])
    cp_h = pltpu.make_async_copy(vhand, out_h, sem_out.at[3])
    loads = [
        pltpu.make_async_copy(got.at[pl.ds(8 * sq, 8)], pieces.at[pl.ds(8 * sq, 8)], sem_in.at[sq])
        for sq in range(2)
    ]
    for cp in loads:
        cp.start()
    in_r.start()
    in_h.start()
    stores = []
    for sq in range(2):
        loads[sq].wait()
        for hh in range(4):
            a = pieces[8 * sq + 2 * hh].astype(F32).reshape(8, 8, 128)
            b = pieces[8 * sq + 2 * hh + 1].astype(F32).reshape(8, 8, 128)
            whole[sq, :, 16 * hh : 16 * hh + 16, :] = jnp.concatenate([a, b], axis=1).astype(BF16)
        cp = pltpu.make_async_copy(whole.at[sq], out_p.at[sq], sem_out.at[sq])
        cp.start()
        stores.append(cp)
    in_r.wait()
    cp_r.start()
    in_h.wait()
    cp_h.start()
    for cp in stores:
        cp.wait()
    cp_r.wait()
    cp_h.wait()


def on_device(
    prompt_lengths, owners, span_q, span_k, span_v, prompt_keys, prompt_values, res_lengths,
    res_keys, res_values, dec_q, dec_k, dec_v, hand_q, hand_k, hand_v,
):
    hbm = pl.BlockSpec(memory_space=pltpu.HBM)
    dma = pltpu.SemaphoreType.DMA
    out = pl.pallas_call(
        kernel,
        out_shape=(
            jax.ShapeDtypeStruct((16, 64, 128), BF16),
            jax.ShapeDtypeStruct((4, 64, 128), BF16),
            jax.ShapeDtypeStruct((4, 16, 128), BF16),
        ),
        in_specs=[hbm] * 16,
        out_specs=(hbm, hbm, hbm),
        scratch_shapes=[
            pltpu.VMEM((2, 8, 64, 128), BF16),
            pltpu.VMEM((2, 8, 8, 128), BF16),
            pltpu.VMEM((2, 8, 8, 128), BF16),
            pltpu.VMEM((2, 128, 128), BF16),
            pltpu.VMEM((2, 128, 128), BF16),
            pltpu.VMEM((4, 2048, 128), BF16),
            pltpu.VMEM((4, 2048, 128), BF16),
            pltpu.SMEM((2,), jnp.int32),
            pltpu.SMEM((2,), jnp.int32),
            pltpu.SMEM((4,), jnp.int32),
            pltpu.VMEM((4, 64, 128), BF16),
            pltpu.VMEM((32, 128), BF16),
            pltpu.VMEM((32, 128), BF16),
            pltpu.VMEM((4, 16, 128), BF16),
            pltpu.VMEM((8, 128), BF16),
            pltpu.VMEM((8, 128), BF16),
            pltpu.VMEM((4, 16, 128), BF16),
            pltpu.VMEM((4, 128, 128), F32),
            pltpu.VMEM((16, 16, 128), BF16),
            pltpu.VMEM((16, 16, 128), BF16),
            pltpu.VMEM((16, 64, 128), BF16),
            pltpu.VMEM((16, 64, 128), BF16),
            pltpu.VMEM((4, 176, 128), BF16),
            pltpu.VMEM((4, 176, 128), BF16),
            pltpu.VMEM((8, 2, 816, 128), BF16),
            pltpu.VMEM((1024, 128), F32),
            pltpu.VMEM((1024, 128), F32),
            pltpu.VMEM((1024, 128), F32),
            pltpu.VMEM((1024, 128), F32),
            pltpu.VMEM((16, 64, 128), BF16),
            pltpu.VMEM((32, 128), BF16),
            pltpu.VMEM((4, 32, 128), BF16),
            pltpu.VMEM((4, 64, 128), BF16),
            pltpu.VMEM((128, 128), BF16),
            pltpu.VMEM((128, 128), BF16),
            dma((14,)), dma((4,)), dma((4,)), dma((2,)),
            dma, dma, dma, dma, dma((4,)), dma, dma((4,)), dma((8, 4)), dma, dma((8,)),
            dma, dma, dma((8,)), dma,
        ],
        compiler_params=pltpu.CompilerParams(
            collective_id=0, has_side_effects=True, vmem_limit_bytes=64 << 20
        ),
        name="spanned",
    )(
        prompt_lengths, owners, res_lengths, span_q, span_k, span_v,
        prompt_keys.reshape(2, 128, 128), prompt_values.reshape(2, 128, 128),
        res_keys.reshape(4, 2048, 128), res_values.reshape(4, 2048, 128),
        dec_q.reshape(4, 64, 128), dec_k.reshape(32, 128), dec_v.reshape(32, 128),
        hand_q.reshape(4, 16, 128), hand_k.reshape(8, 128), hand_v.reshape(8, 128),
    )
    any_space = pl.BlockSpec(memory_space=pl.ANY)
    prefill_out, res_out, hand_out = pl.pallas_call(
        place,
        out_shape=(
            jax.ShapeDtypeStruct((2, 8, 64, 128), BF16),
            jax.ShapeDtypeStruct((4, 64, 128), BF16),
            jax.ShapeDtypeStruct((4, 16, 128), BF16),
        ),
        in_specs=[any_space] * 3,
        out_specs=(any_space,) * 3,
        scratch_shapes=[
            pltpu.VMEM((16, 64, 128), BF16), pltpu.VMEM((2, 8, 64, 128), BF16), pltpu.VMEM((4, 64, 128), BF16),
            pltpu.VMEM((4, 16, 128), BF16), dma((4,)), dma((4,)),
        ],
        compiler_params=pltpu.CompilerParams(vmem_limit_bytes=64 << 20),
        name="place",
    )(*out)
    return (prefill_out, res_out.reshape(4, 4, 16, 128), hand_out.reshape(1, 4, 16, 128))


def solution(mesh):
    cache = P("section", None, "tensor", None)
    span = P(None, ("tensor", "section"), None, None)
    prompt = P(None, "section", "tensor", None)
    return jax.shard_map(
        on_device,
        mesh=mesh,
        in_specs=(P(), P(), span, span, span, prompt, prompt, P("section")) + (cache,) * 8,
        out_specs=(span, cache, cache),
        check_vma=False,
    )
```
